256 devices in a mesh: ctx: 8 (over x, y_lo), ch: 32 (over z, y_hi, core).
Axes of the slice: x: 4, y: 4 (y_hi: 2, y_lo: 2; y = y_hi * 2 + y_lo), z: 8, core: 2. Of those that a mesh axis runs over, the one named last changes fastest.
Arguments:
- out_gate: bfloat16 [4096, 8192], P('ctx', 'ch'), may hold values from -6 to 6
- key_proj: bfloat16 [4096, 8192], P('ctx', 'ch'), may hold values from -6 to 6
- value_proj: bfloat16 [4096, 8192], P('ctx', 'ch'), may hold values from -6 to 6
- filters: float32 [4096, 8192], P('ctx', 'ch'), may hold values from -0.5 to 0.5
- skip_gain: float32 [8192], P('ch'), may hold values from -4 to 4
- out_weight: bfloat16 [8192, 8192], P('ch'), may hold values from -0.125 to 0.125
Outputs:
- projected: bfloat16 [4096, 8192], P('ctx', 'ch')
The draws below stay inside these ranges and needn't reach their ends.
All inputs are finite; a program needn't handle non-finite values.
Results may differ from the reference program's by a relative error of at most 0.02.
Values may be sent and summed in bfloat16 or wider, within the bound.
A program may use at most 128 MiB of HBM per device.

```python
import jax
import jax.numpy as jnp

D = 8192
SEQ = 4096
PADDED = 8192


def spiked(values, key, source, target, parts, factor):
    owner, partner = [(jnp.arange(values.shape[dim]) // (values.shape[dim] // parts)).reshape([-1 if axis == dim else 1 for axis in range(values.ndim)]) for dim in (source, target)]
    chosen = jax.random.permutation(key, parts)[partner]
    strong = (owner == chosen) | (owner == (partner + parts // 2) % parts)
    return jnp.where(strong, factor * values, values)


def levels(key, dims, cuts, low, top_value):
    gain = 1.0
    for axis_at, parts in cuts:
        draws = jax.random.uniform(jax.random.fold_in(jax.random.fold_in(key, 6), axis_at), (parts,), jnp.float32, low / len(cuts), top_value / len(cuts))
        gain = gain * jnp.repeat(jnp.exp(draws), dims[axis_at] // parts).reshape((-1,) + (1,) * (len(dims) - 1 - axis_at))
    return gain


def centred(stream_key, dims, deviation, bound, split=(), held_as=jnp.bfloat16):
    drawn = deviation * jax.random.normal(stream_key, dims, jnp.float32)
    if split:
        drawn = drawn * levels(stream_key, dims, split, -0.22, 0.18)
    return jnp.clip(drawn, -bound, bound).astype(held_as)


def heavy_noise(stream_key, extent, scale, reach, pieces, heavy, held_as=jnp.bfloat16):
    result = scale * jax.random.normal(stream_key, extent, jnp.float32)
    if pieces:
        result = result * levels(stream_key, extent, pieces, -0.22, 0.18)
    return jnp.clip(spiked(result, jax.random.fold_in(stream_key, 3), *heavy), -reach, reach).astype(held_as)


def setup_inputs(seed: int = 0) -> dict:
    seeds = jax.random.split(jax.random.key(seed), 7)
    out_gate = centred(seeds[0], (SEQ, D), 1.0, 6.0, ((0, 8), (1, 32)))
    key_proj = centred(seeds[1], (SEQ, D), 1.0, 6.0, ((0, 8), (1, 32)))
    value_proj = centred(seeds[2], (SEQ, D), 1.0, 6.0, ((0, 8), (1, 32)))
    filters = centred(seeds[3], (SEQ, D), (2.0 / SEQ ** 0.5), 0.5, ((0, 8), (1, 32)), jnp.float32)
    skip_gain = centred(seeds[4], (D,), 1.0, 4.0, ((0, 32),), jnp.float32)
    out_weight = heavy_noise(seeds[5], (D, D), D ** -0.5, 0.125, ((0, 32),), (0, 1, 32, 2.75))
    return dict(out_gate=out_gate, key_proj=key_proj, value_proj=value_proj, filters=filters, skip_gain=skip_gain, out_weight=out_weight)


def reference(out_gate, key_proj, value_proj, filters, skip_gain, out_weight):
    signal = key_proj.astype(jnp.float32) * value_proj.astype(jnp.float32)
    spectrum = jnp.fft.rfft(signal, n=PADDED, axis=0) * jnp.fft.rfft(filters, n=PADDED, axis=0)
    convolved = jnp.fft.irfft(spectrum, n=PADDED, axis=0)[:SEQ]
    gated_act = ((convolved + skip_gain[None, :] * signal) * out_gate.astype(jnp.float32)).astype(jnp.bfloat16)
    return jnp.dot(gated_act, out_weight, preferred_element_type=jnp.float32).astype(jnp.bfloat16)
```

```python
import functools

import jax
import jax.numpy as jnp
import numpy as np
from jax import lax
from jax.experimental import pallas as pl
from jax.experimental.pallas import tpu as pltpu
from jax.sharding import PartitionSpec as P

MESH = pl.DeviceIdType.MESH
F32 = jnp.float32
BF16 = jnp.bfloat16

CTX = 8
POS = 512
CHAN = 256
SUB = CHAN // CTX
BLOCK = 256
BLOCKS = 16
PIECE = 128
RING = 8


def dot(a, b):
    return jnp.dot(a, b, preferred_element_type=F32)


def tables():
    theta = np.pi * (2 * np.arange(BLOCK) + 1) / (2 * BLOCK)
    at = np.arange(-BLOCK, BLOCK)[:, None] * theta[None, :]
    forward = np.concatenate((np.cos(at), -np.sin(at)), axis=1)
    back_at = theta[:, None] * np.arange(BLOCK)[None, :]
    backward = np.concatenate((np.cos(back_at), -np.sin(back_at)), axis=0) / BLOCK
    return jnp.asarray(forward, BF16), jnp.asarray(backward, BF16)


def kernel(
    gate,
    key,
    value,
    filt,
    skip,
    w,
    fwd,
    bwd,
    out,
    tsend,
    trecv,
    sbuf,
    hbuf,
    zbuf,
    csend,
    crecv,
    gall,
    wbuf,
    pbuf,
    rsend,
    rrecv,
    t_ss,
    t_rs,
    c_ss,
    c_rs,
    g_ss,
    g_rs,
    own_s,
    wc_ss,
    wc_rs,
    wy_ss,
    wy_rs,
    wx_ss,
    wx_rs,
    r_ss,
    r_rs,
    loc_s,
):
    i = lax.axis_index("ctx")
    j = lax.axis_index("ch")
    x, lo = i // 2, i % 2
    z, q = j // 4, j % 4
    hi, core = q // 2, q % 2

    def remote(src, dst, ss, rs, device):
        return pltpu.make_async_remote_copy(
            src_ref=src, dst_ref=dst, send_sem=ss, recv_sem=rs, device_id=device, device_id_type=MESH
        )

    def w_cols(far, high, cor):
        at = (((z + far) % RING) * 4 + high * 2 + cor) * CHAN
        return w.at[:, pl.ds(pl.multiple_of(at, CHAN), CHAN)]

    barrier = pltpu.get_barrier_semaphore()
    friends = [((i + d) % CTX, j) for d in range(1, CTX)]
    friends += [(i, z * 4 + (q + d) % 4) for d in range(1, 4)]
    friends += [(i, ((z + d) % RING) * 4 + q) for d in (1, RING - 1)]
    friends += [(x * 2 + 1 - lo, z * 4 + (1 - hi) * 2 + c) for c in range(2)]
    for friend in friends:
        pl.semaphore_signal(barrier, inc=1, device_id=friend, device_id_type=MESH)

    own_w = [pltpu.make_async_copy(w_cols(d, hi, core), wbuf.at[d, q], own_s.at[d]) for d in range(RING)]
    for copy in own_w:
        copy.start()

    signal = key[...].astype(F32) * value[...].astype(F32)
    tsend[0] = signal.T.astype(BF16)
    pl.semaphore_wait(barrier, len(friends))

    def spread(t):
        copies = []
        for d in range(1, CTX):
            to = (i + d) % CTX
            rows = pl.ds(pl.multiple_of(to * SUB, SUB), SUB)
            copy = remote(tsend.at[t, rows], trecv.at[t, i], t_ss.at[t, d - 1], t_rs.at[t, d - 1], (to, j))
            copy.start()
            copies.append(copy)
        rows = pl.ds(pl.multiple_of(i * SUB, SUB), SUB)
        mine = pltpu.make_async_copy(tsend.at[t, rows], trecv.at[t, i], loc_s.at[t])
        mine.start()
        return copies, mine

    sig_copies, sig_mine = spread(0)
    tsend[1] = filt[...].T.astype(BF16)
    fil_copies, fil_mine = spread(1)

    fars = [4 - x, (4 + x) * ((x + 3) // 4)]
    wy = []
    for e in range(2):
        for c in range(2):
            copy = remote(
                w_cols(fars[e], 1 - hi, c),
                wbuf.at[fars[e], q],
                wy_ss.at[e, c],
                wy_rs.at[e, core],
                (x * 2 + 1 - lo, z * 4 + (1 - hi) * 2 + c),
            )
            copy.start()
            wy.append(copy)
    wc = []
    for d in range(RING):
        copy = remote(
            w_cols(d, hi, 1 - core), wbuf.at[d, q], wc_ss.at[d], wc_rs.at[d], (i, z * 4 + hi * 2 + 1 - core)
        )
        copy.start()
        wc.append(copy)

    sig_mine.wait()
    for copy in sig_copies:
        copy.wait_recv()
    for h in range(2):
        lhs = trecv[0, :, :, h * BLOCK : (h + 1) * BLOCK].reshape(CTX * SUB, BLOCK)
        sbuf[h] = dot(lhs, fwd[BLOCK:, :])
    fil_mine.wait()
    for copy in fil_copies:
        copy.wait_recv()
    hbuf[1] = dot(trecv[1].reshape(CTX * SUB, POS), fwd[...])
    hbuf[0] = dot(trecv[1, :, :, :BLOCK].reshape(CTX * SUB, BLOCK), fwd[BLOCK:, :])
    hbuf[0, SUB:, :] += dot(trecv[1, : CTX - 1, :, BLOCK:].reshape((CTX - 1) * SUB, BLOCK), fwd[:BLOCK, :])

    @pl.loop(0, (SUB // 8) * (BLOCK // 128))
    def _(t):
        row0 = (t // 2) * 8
        lane_re = pl.multiple_of((t % 2) * 128, 128)
        lane_im = pl.multiple_of(BLOCK + (t % 2) * 128, 128)

        def take(ref, a):
            rows = pl.ds(pl.multiple_of((a // 2) * SUB + row0, 8), 8)
            return ref[a % 2, rows, pl.ds(lane_re, 128)], ref[a % 2, rows, pl.ds(lane_im, 128)]

        for a in range(BLOCKS):
            re = im = None
            for d in range(a + 1):
                sr, si = take(sbuf, a - d)
                hr, hm = take(hbuf, d)
                pr = sr * hr - si * hm
                pm = sr * hm + si * hr
                re = pr if re is None else re + pr
                im = pm if im is None else im + pm
            rows = pl.ds(pl.multiple_of((a // 2) * SUB + row0, 8), 8)
            zbuf[a % 2, rows, pl.ds(lane_re, 128)] = re
            zbuf[a % 2, rows, pl.ds(lane_im, 128)] = im

    for h in range(2):
        csend[:, h * BLOCK : (h + 1) * BLOCK] = dot(zbuf[h].astype(BF16), bwd[...]).astype(BF16)

    mine_rows = pl.ds(pl.multiple_of(i * SUB, SUB), SUB)
    back = []
    for d in range(1, CTX):
        to = (i + d) % CTX
        rows = pl.ds(pl.multiple_of(to * SUB, SUB), SUB)
        copy = remote(csend.at[rows], crecv.at[mine_rows], c_ss.at[d - 1], c_rs.at[d - 1], (to, j))
        copy.start()
        back.append(copy)
    back_mine = pltpu.make_async_copy(csend.at[mine_rows], crecv.at[mine_rows], loc_s.at[2])
    back_mine.start()

    for e in range(2):
        for c in range(2):
            remote(
                w_cols(fars[e], 1 - hi, c),
                wbuf.at[fars[e], (1 - hi) * 2 + c],
                wy_ss.at[e, c],
                wy_rs.at[e, c],
                (x * 2 + 1 - lo, z * 4 + (1 - hi) * 2 + c),
            ).wait_recv()
    wx = []
    for e in range(2):
        for d in (1, 3, 2):
            block = wbuf.at[fars[e], pl.ds((1 - hi) * 2, 2)]
            copy = remote(block, block, wx_ss.at[e, d - 1], wx_rs.at[e, d - 1], (((x + d) % 4) * 2 + lo, j))
            copy.start()
            wx.append(copy)

    back_mine.wait()
    for copy in back:
        copy.wait_recv()
    convolved = crecv[...].astype(F32).T
    signal = key[...].astype(F32) * value[...].astype(F32)
    gall[q] = ((convolved + skip[...] * signal) * gate[...].astype(F32)).astype(BF16)
    gath = []
    for d in range(1, 4):
        copy = remote(gall.at[q], gall.at[q], g_ss.at[d - 1], g_rs.at[d - 1], (i, z * 4 + (q + d) % 4))
        copy.start()
        gath.append(copy)

    for copy in own_w:
        copy.wait()
    for copy in wc:
        copy.wait_recv()
    for copy in wx:
        copy.wait_recv()
    for copy in gath:
        copy.wait_recv()

    def partial(far):
        total = dot(gall[0], wbuf[far, 0])
        for k in range(1, 4):
            total += dot(gall[k], wbuf[far, k])
        return total

    ways = ((0, 1), (1, RING - 1))
    pieces = POS // PIECE
    sums = {}
    first = partial(4)
    for way, near in ways:
        for r in range(way * pieces // 2, (way + 1) * pieces // 2):
            rows = pl.ds(r * PIECE, PIECE)
            rsend[way, 0, rows] = first[r * PIECE : (r + 1) * PIECE].astype(BF16)
    for step in range(4):
        if step:
            for way, _ in ways:
                pbuf[way] = partial(4 - step if way == 0 else 4 + step)
        for r in range(pieces):
            for way, near in ways:
                rows = pl.ds(r * PIECE, PIECE)
                half = way * pieces // 2 <= r < (way + 1) * pieces // 2
                if step == 0 and not half:
                    continue
                if step:
                    total = pbuf[way, rows]
                    if step > 1 or half:
                        sums[way, step - 1, r].wait_recv()
                        total = total + rrecv[way, step - 1, rows].astype(F32)
                    rsend[way, step, rows] = total.astype(BF16)
                copy = remote(
                    rsend.at[way, step, rows],
                    rrecv.at[way, step, rows],
                    r_ss.at[way, step, r],
                    r_rs.at[way, step, r],
                    (i, ((z + near) % RING) * 4 + q),
                )
                copy.start()
                sums[way, step, r] = copy
    pbuf[0] = partial(0)
    for r in range(pieces):
        rows = pl.ds(r * PIECE, PIECE)
        total = pbuf[0, rows]
        for way, _ in ways:
            sums[way, 3, r].wait_recv()
            total = total + rrecv[way, 3, rows].astype(F32)
        out[rows, :] = total.astype(BF16)

    for copy in sig_copies + fil_copies + wy + wc + back + wx + gath + list(sums.values()):
        copy.wait_send()


def body(gate, key, value, filt, skip, w, fwd, bwd):
    vmem = pl.BlockSpec(memory_space=pltpu.VMEM)
    dma = pltpu.SemaphoreType.DMA
    return pl.pallas_call(
        kernel,
        out_shape=jax.ShapeDtypeStruct((POS, CHAN), BF16),
        in_specs=[vmem] * 5 + [pl.BlockSpec(memory_space=pl.ANY)] + [vmem] * 2,
        out_specs=vmem,
        scratch_shapes=[
            pltpu.VMEM((2, CHAN, POS), BF16),
            pltpu.VMEM((2, CTX, SUB, POS), BF16),
            pltpu.VMEM((2, CHAN, 2 * BLOCK), F32),
            pltpu.VMEM((2, CHAN, 2 * BLOCK), F32),
            pltpu.VMEM((2, CHAN, 2 * BLOCK), F32),
            pltpu.VMEM((CHAN, POS), BF16),
            pltpu.VMEM((CHAN, POS), BF16),
            pltpu.VMEM((4, POS, CHAN), BF16),
            pltpu.VMEM((RING, 4, CHAN, CHAN), BF16),
            pltpu.VMEM((2, POS, CHAN), F32),
            pltpu.VMEM((2, 4, POS, CHAN), BF16),
            pltpu.VMEM((2, 4, POS, CHAN), BF16),
            dma((2, CTX - 1)),
            dma((2, CTX - 1)),
            dma((CTX - 1,)),
            dma((CTX - 1,)),
            dma((3,)),
            dma((3,)),
            dma((RING,)),
            dma((RING,)),
            dma((RING,)),
            dma((2, 2)),
            dma((2, 2)),
            dma((2, 3)),
            dma((2, 3)),
            dma((2, 4, POS // PIECE)),
            dma((2, 4, POS // PIECE)),
            dma((3,)),
        ],
        compiler_params=pltpu.CompilerParams(
            collective_id=0, has_side_effects=True, vmem_limit_bytes=40 * 1024 * 1024
        ),
        name="hyena",
    )(gate, key, value, filt, skip.reshape(1, CHAN), w, fwd, bwd)


def solution(mesh):
    mapped = jax.shard_map(
        body,
        mesh=mesh,
        in_specs=(P("ctx", "ch"),) * 4 + (P("ch"), P("ch", None), P(), P()),
        out_specs=P("ctx", "ch"),
        check_vma=False,
    )

    def run(out_gate, key_proj, value_proj, filters, skip_gain, out_weight):
        return mapped(out_gate, key_proj, value_proj, filters, skip_gain, out_weight, *tables())

    return run
```

```python
import functools

import jax
import jax.numpy as jnp
import numpy as np
from jax import lax
from jax.experimental import pallas as pl
from jax.experimental.pallas import tpu as pltpu
from jax.sharding import PartitionSpec as P

MESH = pl.DeviceIdType.MESH
F32 = jnp.float32
BF16 = jnp.bfloat16

CTX = 8
POS = 512
CHAN = 256
SUB = CHAN // CTX
BLOCK = 256
BLOCKS = 16
PIECE = 128
RING = 8
ORDER = (4, 3, 5, 2, 6, 1, 7, 0)
SHARE = CHAN // 4


def dot(a, b):
    return jnp.dot(a, b, preferred_element_type=F32)


class Move:
    def __init__(self, copy, log):
        self.copy, self.landed, self.remote = copy, False, copy.is_remote
        copy.start()
        log.append(self)

    def land(self):
        self.landed = True
        if self.remote:
            self.copy.wait_recv()
        else:
            self.copy.wait()

    def leave(self):
        if self.remote:
            self.copy.wait_send()


def tables():
    theta = np.pi * (2 * np.arange(BLOCK) + 1) / (2 * BLOCK)
    at = np.arange(-BLOCK, BLOCK)[:, None] * theta[None, :]
    forward = np.concatenate((np.cos(at), -np.sin(at)), axis=1)
    back_at = theta[:, None] * np.arange(BLOCK)[None, :]
    backward = np.concatenate((np.cos(back_at), -np.sin(back_at)), axis=0) / BLOCK
    return jnp.asarray(forward, BF16), jnp.asarray(backward, BF16)


def kernel(
    gate_h,
    key_h,
    value_h,
    filt_h,
    skip,
    w,
    fwd_h,
    bwd_h,
    out,
    gate,
    key,
    value,
    filt,
    fwd,
    bwd,
    tsend,
    trecv,
    sbuf,
    hbuf,
    zbuf,
    csend,
    crecv,
    gall,
    wbuf,
    rsend,
    rrecv,
    t_ss,
    t_rs,
    c_ss,
    c_rs,
    g_ss,
    g_rs,
    own_s,
    wc_ss,
    wc_rs,
    wy_ss,
    wy_rs,
    wx_ss,
    wx_rs,
    r_ss,
    r_rs,
    loc_s,
    in_s,
):
    log = []
    i = lax.axis_index("ctx")
    j = lax.axis_index("ch")
    x, lo = i // 2, i % 2
    z, q = j // 4, j % 4
    hi, core = q // 2, q % 2

    def remote(src, dst, ss, rs, device):
        copy = pltpu.make_async_remote_copy(
            src_ref=src, dst_ref=dst, send_sem=ss, recv_sem=rs, device_id=device, device_id_type=MESH
        )
        return Move(copy, log)

    def local(src, dst, sem):
        return Move(pltpu.make_async_copy(src, dst, sem), log)

    pairs = ((key_h, key), (value_h, value), (filt_h, filt), (fwd_h, fwd), (bwd_h, bwd), (gate_h, gate))
    key_in, value_in, filt_in, fwd_in, bwd_in, gate_in = [
        local(src, dst, in_s.at[n]) for n, (src, dst) in enumerate(pairs)
    ]

    share = pl.ds(pl.multiple_of(x * SHARE, SHARE), SHARE)

    def w_cols(n, high, cor, rows):
        at = (((z + ORDER[n]) % RING) * 4 + high * 2 + cor) * CHAN
        return w.at[rows, pl.ds(pl.multiple_of(at, CHAN), CHAN)]

    barrier = pltpu.get_barrier_semaphore()
    friends = [((i + d) % CTX, j) for d in range(1, CTX)]
    sibling = (i, z * 4 + hi * 2 + 1 - core)
    across = (i, z * 4 + (q + 2) % 4)
    friends += [sibling, across]
    friends += [(i, ((z + d) % RING) * 4 + q) for d in (1, RING - 1)]
    friends += [(x * 2 + 1 - lo, z * 4 + (1 - hi) * 2 + c) for c in range(2)]
    for friend in friends:
        pl.semaphore_signal(barrier, inc=1, device_id=friend, device_id_type=MESH)

    key_in.land()
    value_in.land()
    signal = key[...].astype(F32) * value[...].astype(F32)
    tsend[0] = signal.T.astype(BF16)
    pl.semaphore_wait(barrier, len(friends))

    def spread(t):
        copies = []
        for d in range(1, CTX):
            to = (i + d) % CTX
            rows = pl.ds(pl.multiple_of(to * SUB, SUB), SUB)
            copies.append(remote(tsend.at[t, rows], trecv.at[t, i], t_ss.at[t, d - 1], t_rs.at[t, d - 1], (to, j)))
        rows = pl.ds(pl.multiple_of(i * SUB, SUB), SUB)
        copies.append(local(tsend.at[t, rows], trecv.at[t, i], loc_s.at[t]))
        return copies

    sig_copies = spread(0)
    filt_in.land()
    tsend[1] = filt[...].T.astype(BF16)
    fil_copies = spread(1)

    wy, wc, own_w = [], [], []
    for n in range(RING):
        both = []
        for m in range(2):
            c = (core + m) % 2
            target = (x * 2 + 1 - lo, z * 4 + (1 - hi) * 2 + c)
            src = w_cols(n, 1 - hi, c, share)
            both.append(remote(src, wbuf.at[n, q, share], wy_ss.at[n, m], wy_rs.at[n, m], target))
        wy.append(both)
    every = pl.ds(0, CHAN)
    for n in range(RING):
        own_w.append(local(w_cols(n, hi, core, every), wbuf.at[n, q], own_s.at[n]))
        wc.append(remote(w_cols(n, hi, 1 - core, every), wbuf.at[n, q], wc_ss.at[n], wc_rs.at[n], sibling))
    wx = {}

    def along_x(g, first, last):
        for n in range(first, last):
            for copy in wy[n]:
                copy.land()
        block = wbuf.at[pl.ds(first, last - first), pl.ds((1 - hi) * 2, 2), share]
        for d in (1, 3, 2):
            target = (((x + d) % 4) * 2 + lo, j)
            copy = remote(block, block, wx_ss.at[g, d - 1], wx_rs.at[g, d - 1], target)
            for n in range(first, last):
                wx.setdefault(n, []).append(copy)

    fwd_in.land()
    for copy in sig_copies:
        copy.land()
    for h in range(2):
        lhs = trecv[0, :, :, h * BLOCK : (h + 1) * BLOCK].reshape(CTX * SUB, BLOCK)
        sbuf[h] = dot(lhs, fwd[BLOCK:, :])
    for copy in fil_copies:
        copy.land()
    hbuf[1] = dot(trecv[1].reshape(CTX * SUB, POS), fwd[...])
    hbuf[0] = dot(trecv[1, :, :, :BLOCK].reshape(CTX * SUB, BLOCK), fwd[BLOCK:, :])
    hbuf[0, SUB:, :] += dot(trecv[1, : CTX - 1, :, BLOCK:].reshape((CTX - 1) * SUB, BLOCK), fwd[:BLOCK, :])

    along_x(0, 0, 1)
    bwd_in.land()
    mine_rows = pl.ds(pl.multiple_of(i * SUB, SUB), SUB)
    back = []
    for h in range(2):
        @pl.loop(0, (SUB // 8) * (BLOCK // 128))
        def _(t):
            row0 = (t // 2) * 8
            lane_re = pl.multiple_of((t % 2) * 128, 128)
            lane_im = pl.multiple_of(BLOCK + (t % 2) * 128, 128)

            def at(a):
                return pl.ds(pl.multiple_of((a // 2) * SUB + row0, 8), 8)

            def take(ref, a):
                return ref[a % 2, at(a), pl.ds(lane_re, 128)], ref[a % 2, at(a), pl.ds(lane_im, 128)]

            for a in range(h, BLOCKS, 2):
                re = im = None
                for d in range(a + 1):
                    sr, si = take(sbuf, a - d)
                    hr, hm = take(hbuf, d)
                    pr = sr * hr - si * hm
                    pm = sr * hm + si * hr
                    re = pr if re is None else re + pr
                    im = pm if im is None else im + pm
                zbuf[h, at(a), pl.ds(lane_re, 128)] = re
                zbuf[h, at(a), pl.ds(lane_im, 128)] = im

        csend[h] = dot(zbuf[h].astype(BF16), bwd[...]).astype(BF16)
        copies = []
        for d in range(1, CTX):
            to = (i + d) % CTX
            rows = pl.ds(pl.multiple_of(to * SUB, SUB), SUB)
            copies.append(
                remote(csend.at[h, rows], crecv.at[h, mine_rows], c_ss.at[h, d - 1], c_rs.at[h, d - 1], (to, j))
            )
        copies.append(local(csend.at[h, mine_rows], crecv.at[h, mine_rows], loc_s.at[2 + h]))
        back.append(copies)

    gate_in.land()
    cross, beside, passed = [], [], []
    for h in range(2):
        rows = pl.ds(h * BLOCK, BLOCK)
        for copy in back[h]:
            copy.land()
        convolved = crecv[h].astype(F32).T
        signal = key[rows, :].astype(F32) * value[rows, :].astype(F32)
        gall[q, rows] = ((convolved + skip[...] * signal) * gate[rows, :].astype(F32)).astype(BF16)
        block = gall.at[q, rows]
        cross.append(remote(block, block, g_ss.at[h, 0], g_rs.at[h, 0], across))
        beside.append(remote(block, block, g_ss.at[h, 1], g_rs.at[h, 1], sibling))
    along_x(1, 1, 3)

    def gathered(h):
        cross[h].land()
        block = gall.at[(q + 2) % 4, pl.ds(h * BLOCK, BLOCK)]
        passed.append(remote(block, block, g_ss.at[h, 2], g_rs.at[h, 2], sibling))
        beside[h].land()
        passed[h].land()

    ready = set()

    def partial(far, r):
        n = ORDER.index(far)
        if n not in ready:
            ready.add(n)
            for copy in [own_w[n], wc[n]] + wx[n]:
                if not copy.landed:
                    copy.land()
        rows = slice(r * PIECE, (r + 1) * PIECE)
        total = dot(gall[0, rows], wbuf[n, 0])
        for k in range(1, 4):
            total += dot(gall[k, rows], wbuf[n, k])
        return total

    turns = []
    for way in range(2):
        near, far = (way, 2 + way), (1 - way, 3 - way)
        turn = [(0, near[0]), (1, far[0]), (0, near[1]), (1, far[1]), (1, near[0]), (1, near[1])]
        for step in (2, 3):
            turn += [(step, r) for r in far + near]
        turns.append(turn)
    sums = {}
    for n in range(len(turns[0])):
        if n == 0:
            gathered(0)
        if n == 2:
            gathered(1)
            along_x(2, 3, 5)
        if n == 6:
            along_x(3, 5, 8)
        for way, near in ((0, 1), (1, RING - 1)):
            step, r = turns[way][n]
            rows = pl.ds(r * PIECE, PIECE)
            total = partial(4 - step if way == 0 else 4 + step, r)
            if (way, step - 1, r) in sums:
                sums[way, step - 1, r].land()
                total = total + rrecv[way, step - 1, rows].astype(F32)
            rsend[way, step, rows] = total.astype(BF16)
            sums[way, step, r] = remote(
                rsend.at[way, step, rows],
                rrecv.at[way, step, rows],
                r_ss.at[way, step, r],
                r_rs.at[way, step, r],
                (i, ((z + near) % RING) * 4 + q),
            )
    for r in range(POS // PIECE):
        rows = pl.ds(r * PIECE, PIECE)
        total = partial(0, r)
        for way in range(2):
            sums[way, 3, r].land()
            total = total + rrecv[way, 3, rows].astype(F32)
        out[rows, :] = total.astype(BF16)

    for copy in log:
        copy.leave()


def body(gate, key, value, filt, skip, w, fwd, bwd):
    vmem = pl.BlockSpec(memory_space=pltpu.VMEM)
    hbm = pl.BlockSpec(memory_space=pltpu.HBM)
    dma = pltpu.SemaphoreType.DMA
    return pl.pallas_call(
        kernel,
        out_shape=jax.ShapeDtypeStruct((POS, CHAN), BF16),
        in_specs=[hbm] * 4 + [vmem] + [hbm] * 3,
        out_specs=vmem,
        scratch_shapes=[
            pltpu.VMEM((POS, CHAN), BF16),
            pltpu.VMEM((POS, CHAN), BF16),
            pltpu.VMEM((POS, CHAN), BF16),
            pltpu.VMEM((POS, CHAN), F32),
            pltpu.VMEM((2 * BLOCK, 2 * BLOCK), BF16),
            pltpu.VMEM((2 * BLOCK, BLOCK), BF16),
            pltpu.VMEM((2, CHAN, POS), BF16),
            pltpu.VMEM((2, CTX, SUB, POS), BF16),
            pltpu.VMEM((2, CHAN, 2 * BLOCK), F32),
            pltpu.VMEM((2, CHAN, 2 * BLOCK), F32),
            pltpu.VMEM((2, CHAN, 2 * BLOCK), F32),
            pltpu.VMEM((2, CHAN, BLOCK), BF16),
            pltpu.VMEM((2, CHAN, BLOCK), BF16),
            pltpu.VMEM((4, POS, CHAN), BF16),
            pltpu.VMEM((RING, 4, CHAN, CHAN), BF16),
            pltpu.VMEM((2, 4, POS, CHAN), BF16),
            pltpu.VMEM((2, 4, POS, CHAN), BF16),
            dma((2, CTX - 1)),
            dma((2, CTX - 1)),
            dma((2, CTX - 1)),
            dma((2, CTX - 1)),
            dma((2, 3)),
            dma((2, 3)),
            dma((RING,)),
            dma((RING,)),
            dma((RING,)),
            dma((RING, 2)),
            dma((RING, 2)),
            dma((4, 3)),
            dma((4, 3)),
            dma((2, 4, POS // PIECE)),
            dma((2, 4, POS // PIECE)),
            dma((4,)),
            dma((6,)),
        ],
        compiler_params=pltpu.CompilerParams(
            collective_id=0, has_side_effects=True, vmem_limit_bytes=64 * 1024 * 1024
        ),
        name="hyena",
    )(gate, key, value, filt, skip.reshape(1, CHAN), w, fwd, bwd)


def solution(mesh):
    mapped = jax.shard_map(
        body,
        mesh=mesh,
        in_specs=(P("ctx", "ch"),) * 4 + (P("ch"), P("ch", None), P(), P()),
        out_specs=P("ctx", "ch"),
        check_vma=False,
    )

    def run(out_gate, key_proj, value_proj, filters, skip_gain, out_weight):
        return mapped(out_gate, key_proj, value_proj, filters, skip_gain, out_weight, *tables())

    return run
```

```python
import functools

import jax
import jax.numpy as jnp
import numpy as np
from jax import lax
from jax.experimental import pallas as pl
from jax.experimental.pallas import tpu as pltpu
from jax.sharding import PartitionSpec as P

MESH = pl.DeviceIdType.MESH
F32 = jnp.float32
BF16 = jnp.bfloat16

CTX = 8
POS = 512
CHAN = 256
SUB = CHAN // CTX
BLOCK = 256
BLOCKS = 16
PIECE = 128
RING = 8
ORDER = (4, 3, 5, 2, 6, 1, 7, 0)
SHARE = CHAN // 4
TWICE = (1, 2)


def dot(a, b):
    return jnp.dot(a, b, preferred_element_type=F32)


class Move:
    def __init__(self, copy, log):
        self.copy, self.landed, self.remote = copy, False, copy.is_remote
        copy.start()
        log.append(self)

    def land(self):
        self.landed = True
        if self.remote:
            self.copy.wait_recv()
        else:
            self.copy.wait()

    def leave(self):
        if self.remote:
            self.copy.wait_send()


def tables():
    theta = np.pi * (2 * np.arange(BLOCK) + 1) / (2 * BLOCK)
    at = np.arange(-BLOCK, BLOCK)[:, None] * theta[None, :]
    forward = np.concatenate((np.cos(at), -np.sin(at)), axis=1)
    back_at = theta[:, None] * np.arange(BLOCK)[None, :]
    backward = np.concatenate((np.cos(back_at), -np.sin(back_at)), axis=0) / BLOCK
    return jnp.asarray(forward, BF16), jnp.asarray(backward, BF16)


def kernel(
    gate_h,
    key_h,
    value_h,
    filt_h,
    skip,
    w_h,
    fwd_h,
    bwd_h,
    out,
    gate,
    key,
    value,
    filt,
    fwd,
    bwd,
    w,
    tsend,
    trecv,
    sbuf,
    hbuf,
    zbuf,
    csend,
    crecv,
    gall,
    wbuf,
    pbuf,
    rsend,
    rrecv,
    t_ss,
    t_rs,
    c_ss,
    c_rs,
    g_ss,
    g_rs,
    wc_ss,
    wc_rs,
    wy_ss,
    wy_rs,
    wx_ss,
    wx_rs,
    r_ss,
    r_rs,
    loc_s,
    in_s,
):
    log = []
    i = lax.axis_index("ctx")
    j = lax.axis_index("ch")
    x, lo = i // 2, i % 2
    z, q = j // 4, j % 4
    hi, core = q // 2, q % 2

    def remote(src, dst, ss, rs, device):
        copy = pltpu.make_async_remote_copy(
            src_ref=src, dst_ref=dst, send_sem=ss, recv_sem=rs, device_id=device, device_id_type=MESH
        )
        return Move(copy, log)

    def local(src, dst, sem):
        return Move(pltpu.make_async_copy(src, dst, sem), log)

    pairs = ((key_h, key), (value_h, value), (filt_h, filt), (fwd_h, fwd), (bwd_h, bwd), (gate_h, gate), (w_h, w))
    key_in, value_in, filt_in, fwd_in, bwd_in, gate_in, w_in = [
        local(src, dst, in_s.at[n]) for n, (src, dst) in enumerate(pairs)
    ]

    shares = [pl.ds(pl.multiple_of((x + d) % 4 * SHARE, SHARE), SHARE) for d in range(2)]

    def w_cols(n, high, cor, rows):
        at = (((z + ORDER[n]) % RING) * 4 + high * 2 + cor) * CHAN
        return w.at[rows, pl.ds(pl.multiple_of(at, CHAN), CHAN)]

    barrier = pltpu.get_barrier_semaphore()
    friends = [((i + d) % CTX, j) for d in range(1, CTX)]
    sibling = (i, z * 4 + hi * 2 + 1 - core)
    across = (i, z * 4 + (q + 2) % 4)
    friends += [sibling, across]
    friends += [(i, ((z + d) % RING) * 4 + q) for d in (1, RING - 1)]
    friends += [(x * 2 + 1 - lo, z * 4 + (1 - hi) * 2 + c) for c in range(2)]
    for friend in friends:
        pl.semaphore_signal(barrier, inc=1, device_id=friend, device_id_type=MESH)

    key_in.land()
    value_in.land()
    signal = key[...].astype(F32) * value[...].astype(F32)
    tsend[0] = signal.T.astype(BF16)
    pl.semaphore_wait(barrier, len(friends))

    def spread(t):
        copies = []
        for d in range(1, CTX):
            to = (i + d) % CTX
            rows = pl.ds(pl.multiple_of(to * SUB, SUB), SUB)
            copies.append(remote(tsend.at[t, rows], trecv.at[t, i], t_ss.at[t, d - 1], t_rs.at[t, d - 1], (to, j)))
        rows = pl.ds(pl.multiple_of(i * SUB, SUB), SUB)
        copies.append(local(tsend.at[t, rows], trecv.at[t, i], loc_s.at[t]))
        return copies

    sig_copies = spread(0)
    filt_in.land()
    tsend[1] = filt[...].T.astype(BF16)
    fil_copies = spread(1)

    w_in.land()
    wy, wc = {}, []

    def along_y(first, last):
        for n in range(first, last):
            wy[n] = []
            for m in range(2):
                c = (core + m) % 2
                target = (x * 2 + 1 - lo, z * 4 + (1 - hi) * 2 + c)
                for d, rows in enumerate(shares if n in TWICE else shares[:1]):
                    src = w_cols(n, 1 - hi, c, rows)
                    wy[n].append(remote(src, wbuf.at[n, q, rows], wy_ss.at[n, m, d], wy_rs.at[n, m, d], target))

    along_y(0, RING)
    every = pl.ds(0, CHAN)
    wx = {}

    def along_x(g, first, last):
        for n in range(first, last):
            for copy in wy[n]:
                copy.land()
        if first in TWICE:
            plan = ((1, shares[0]), (3, shares[1]))
        else:
            plan = ((1, shares[0]), (3, shares[0]), (2, shares[0]))
        for d, rows in plan:
            block = wbuf.at[pl.ds(first, last - first), pl.ds((1 - hi) * 2, 2), rows]
            target = (((x + d) % 4) * 2 + lo, j)
            copy = remote(block, block, wx_ss.at[g, d - 1], wx_rs.at[g, d - 1], target)
            for n in range(first, last):
                wx.setdefault(n, []).append(copy)

    fwd_in.land()
    for copy in sig_copies:
        copy.land()
    for h in range(2):
        lhs = trecv[0, :, :, h * BLOCK : (h + 1) * BLOCK].reshape(CTX * SUB, BLOCK)
        sbuf[h] = dot(lhs, fwd[BLOCK:, :])
    for copy in fil_copies:
        copy.land()
    hbuf[1] = dot(trecv[1].reshape(CTX * SUB, POS), fwd[...])
    hbuf[0] = dot(trecv[1, :, :, :BLOCK].reshape(CTX * SUB, BLOCK), fwd[BLOCK:, :])
    hbuf[0, SUB:, :] += dot(trecv[1, : CTX - 1, :, BLOCK:].reshape((CTX - 1) * SUB, BLOCK), fwd[:BLOCK, :])

    along_x(0, 0, 1)
    bwd_in.land()
    mine_rows = pl.ds(pl.multiple_of(i * SUB, SUB), SUB)
    back = []
    for h in range(2):
        @pl.loop(0, (SUB // 8) * (BLOCK // 128))
        def _(t):
            row0 = (t // 2) * 8
            lane_re = pl.multiple_of((t % 2) * 128, 128)
            lane_im = pl.multiple_of(BLOCK + (t % 2) * 128, 128)

            def at(a):
                return pl.ds(pl.multiple_of((a // 2) * SUB + row0, 8), 8)

            def take(ref, a):
                return ref[a % 2, at(a), pl.ds(lane_re, 128)], ref[a % 2, at(a), pl.ds(lane_im, 128)]

            for a in range(h, BLOCKS, 2):
                re = im = None
                for d in range(a + 1):
                    sr, si = take(sbuf, a - d)
                    hr, hm = take(hbuf, d)
                    pr = sr * hr - si * hm
                    pm = sr * hm + si * hr
                    re = pr if re is None else re + pr
                    im = pm if im is None else im + pm
                zbuf[h, at(a), pl.ds(lane_re, 128)] = re
                zbuf[h, at(a), pl.ds(lane_im, 128)] = im

        csend[h] = dot(zbuf[h].astype(BF16), bwd[...]).astype(BF16)
        copies = []
        for d in range(1, CTX):
            to = (i + d) % CTX
            rows = pl.ds(pl.multiple_of(to * SUB, SUB), SUB)
            copies.append(
                remote(csend.at[h, rows], crecv.at[h, mine_rows], c_ss.at[h, d - 1], c_rs.at[h, d - 1], (to, j))
            )
        copies.append(local(csend.at[h, mine_rows], crecv.at[h, mine_rows], loc_s.at[2 + h]))
        back.append(copies)

    for n in range(RING):
        wc.append(remote(w_cols(n, hi, 1 - core, every), wbuf.at[n, q], wc_ss.at[n], wc_rs.at[n], sibling))

    gate_in.land()
    cross, beside, passed = [], [], []
    for h in range(2):
        rows = pl.ds(h * BLOCK, BLOCK)
        for copy in back[h]:
            copy.land()
        convolved = crecv[h].astype(F32).T
        signal = key[rows, :].astype(F32) * value[rows, :].astype(F32)
        gall[q, rows] = ((convolved + skip[...] * signal) * gate[rows, :].astype(F32)).astype(BF16)
        block = gall.at[q, rows]
        cross.append(remote(block, block, g_ss.at[h, 0], g_rs.at[h, 0], across))
        beside.append(remote(block, block, g_ss.at[h, 1], g_rs.at[h, 1], sibling))
    along_x(1, 1, 3)
    along_x(2, 3, 5)
    along_x(3, 5, 8)

    def gathered(h):
        cross[h].land()
        block = gall.at[(q + 2) % 4, pl.ds(h * BLOCK, BLOCK)]
        passed.append(remote(block, block, g_ss.at[h, 2], g_rs.at[h, 2], sibling))
        beside[h].land()
        passed[h].land()

    ready = set()

    def partial(far, first, count):
        n = ORDER.index(far)
        if n not in ready:
            ready.add(n)
            for copy in [wc[n]] + wx[n]:
                if not copy.landed:
                    copy.land()
        rows = pl.ds(first, count)
        total = dot(gall[q, rows], w_cols(n, hi, core, every)[...])
        for k in range(1, 4):
            at = (q + k) % 4
            total += dot(gall[at, rows], wbuf[n, at])
        pbuf[n, rows] = total

    turns = []
    for way in range(2):
        near, far = (way, 2 + way), (1 - way, 3 - way)
        turn = [(0, near[0]), (1, far[0]), (0, near[1]), (1, far[1]), (1, near[0]), (1, near[1])]
        for step in (2, 3):
            turn += [(step, r) for r in far + near]
        turns.append(turn)
    sums = {}
    ahead = {4: (2,), 6: (6,), 8: (1,), 10: (7,), 12: (0,)}
    for n in range(len(turns[0])):
        if n in (0, 2):
            gathered(n // 2)
            partial(4, n // 2 * BLOCK, BLOCK)
        for far in ahead.get(n, ()):
            partial(far, 0, POS)
        for way, near in ((0, 1), (1, RING - 1)):
            step, r = turns[way][n]
            far = 4 - step if way == 0 else 4 + step
            if n in (1, 3):
                partial(far, n // 2 * BLOCK, BLOCK)
            rows = pl.ds(r * PIECE, PIECE)
            total = pbuf[ORDER.index(far), rows]
            if (way, step - 1, r) in sums:
                sums[way, step - 1, r].land()
                total = total + rrecv[way, step - 1, rows].astype(F32)
            rsend[way, step, rows] = total.astype(BF16)
            sums[way, step, r] = remote(
                rsend.at[way, step, rows],
                rrecv.at[way, step, rows],
                r_ss.at[way, step, r],
                r_rs.at[way, step, r],
                (i, ((z + near) % RING) * 4 + q),
            )
    for r in (1, 3, 0, 2):
        rows = pl.ds(r * PIECE, PIECE)
        total = pbuf[ORDER.index(0), rows]
        for way in range(2):
            sums[way, 3, r].land()
            total = total + rrecv[way, 3, rows].astype(F32)
        out[rows, :] = total.astype(BF16)

    for copy in log:
        copy.leave()


def body(gate, key, value, filt, skip, w, fwd, bwd):
    vmem = pl.BlockSpec(memory_space=pltpu.VMEM)
    hbm = pl.BlockSpec(memory_space=pltpu.HBM)
    dma = pltpu.SemaphoreType.DMA
    return pl.pallas_call(
        kernel,
        out_shape=jax.ShapeDtypeStruct((POS, CHAN), BF16),
        in_specs=[hbm] * 4 + [vmem] + [hbm] * 3,
        out_specs=vmem,
        scratch_shapes=[
            pltpu.VMEM((POS, CHAN), BF16),
            pltpu.VMEM((POS, CHAN), BF16),
            pltpu.VMEM((POS, CHAN), BF16),
            pltpu.VMEM((POS, CHAN), F32),
            pltpu.VMEM((2 * BLOCK, 2 * BLOCK), BF16),
            pltpu.VMEM((2 * BLOCK, BLOCK), BF16),
            pltpu.VMEM((CHAN, RING * 4 * CHAN), BF16),
            pltpu.VMEM((2, CHAN, POS), BF16),
            pltpu.VMEM((2, CTX, SUB, POS), BF16),
            pltpu.VMEM((2, CHAN, 2 * BLOCK), F32),
            pltpu.VMEM((2, CHAN, 2 * BLOCK), F32),
            pltpu.VMEM((2, CHAN, 2 * BLOCK), F32),
            pltpu.VMEM((2, CHAN, BLOCK), BF16),
            pltpu.VMEM((2, CHAN, BLOCK), BF16),
            pltpu.VMEM((4, POS, CHAN), BF16),
            pltpu.VMEM((RING, 4, CHAN, CHAN), BF16),
            pltpu.VMEM((RING, POS, CHAN), F32),
            pltpu.VMEM((2, 4, POS, CHAN), BF16),
            pltpu.VMEM((2, 4, POS, CHAN), BF16),
            dma((2, CTX - 1)),
            dma((2, CTX - 1)),
            dma((2, CTX - 1)),
            dma((2, CTX - 1)),
            dma((2, 3)),
            dma((2, 3)),
            dma((RING,)),
            dma((RING,)),
            dma((RING, 2, 2)),
            dma((RING, 2, 2)),
            dma((4, 3)),
            dma((4, 3)),
            dma((2, 4, POS // PIECE)),
            dma((2, 4, POS // PIECE)),
            dma((4,)),
            dma((7,)),
        ],
        compiler_params=pltpu.CompilerParams(
            collective_id=0, has_side_effects=True, vmem_limit_bytes=64 * 1024 * 1024
        ),
        name="hyena",
    )(gate, key, value, filt, skip.reshape(1, CHAN), w, fwd, bwd)


def solution(mesh):
    mapped = jax.shard_map(
        body,
        mesh=mesh,
        in_specs=(P("ctx", "ch"),) * 4 + (P("ch"), P("ch", None), P(), P()),
        out_specs=P("ctx", "ch"),
        check_vma=False,
    )

    def run(out_gate, key_proj, value_proj, filters, skip_gain, out_weight):
        return mapped(out_gate, key_proj, value_proj, filters, skip_gain, out_weight, *tables())

    return run
```

```python
import functools

import jax
import jax.numpy as jnp
import numpy as np
from jax import lax
from jax.experimental import pallas as pl
from jax.experimental.pallas import tpu as pltpu
from jax.sharding import PartitionSpec as P

MESH = pl.DeviceIdType.MESH
F32 = jnp.float32
BF16 = jnp.bfloat16

CTX = 8
POS = 512
CHAN = 256
FARTHEST = (4, 5, 3, 2, 6, 1, 7)
SUB = CHAN // CTX
BLOCK = 256
BLOCKS = 16
PIECE = 128
RING = 8
ORDER = (4, 3, 5, 2, 6, 1, 7, 0)
SHARE = CHAN // 4
TWICE = (1, 2)


def dot(a, b):
    return jnp.dot(a, b, preferred_element_type=F32)


class Move:
    def __init__(self, copy, log):
        self.copy, self.landed, self.remote = copy, False, copy.is_remote
        copy.start()
        log.append(self)

    def land(self):
        self.landed = True
        if self.remote:
            self.copy.wait_recv()
        else:
            self.copy.wait()

    def leave(self):
        if self.remote:
            self.copy.wait_send()


def tables():
    theta = np.pi * (2 * np.arange(BLOCK) + 1) / (2 * BLOCK)
    at = np.arange(-BLOCK, BLOCK)[:, None] * theta[None, :]
    forward = np.concatenate((np.cos(at), -np.sin(at)), axis=1)
    back_at = theta[:, None] * np.arange(BLOCK)[None, :]
    backward = np.concatenate((np.cos(back_at), -np.sin(back_at)), axis=0) / BLOCK
    return jnp.asarray(forward, BF16), jnp.asarray(backward, BF16)


def kernel(
    gate_h,
    key_h,
    value_h,
    filt_h,
    skip,
    w_h,
    fwd_h,
    bwd_h,
    out,
    gate,
    key,
    value,
    filt,
    fwd,
    bwd,
    w,
    tsend,
    trecv,
    sbuf,
    hbuf,
    zbuf,
    csend,
    crecv,
    gall,
    wbuf,
    pbuf,
    rsend,
    rrecv,
    t_ss,
    t_rs,
    c_ss,
    c_rs,
    g_ss,
    g_rs,
    wc_ss,
    wc_rs,
    wy_ss,
    wy_rs,
    wx_ss,
    wx_rs,
    r_ss,
    r_rs,
    loc_s,
    in_s,
):
    log = []
    i = lax.axis_index("ctx")
    j = lax.axis_index("ch")
    x, lo = i // 2, i % 2
    z, q = j // 4, j % 4
    hi, core = q // 2, q % 2

    def remote(src, dst, ss, rs, device):
        copy = pltpu.make_async_remote_copy(
            src_ref=src, dst_ref=dst, send_sem=ss, recv_sem=rs, device_id=device, device_id_type=MESH
        )
        return Move(copy, log)

    def local(src, dst, sem):
        return Move(pltpu.make_async_copy(src, dst, sem), log)

    pairs = ((key_h, key), (value_h, value), (filt_h, filt), (fwd_h, fwd), (bwd_h, bwd), (gate_h, gate), (w_h, w))
    key_in, value_in, filt_in, fwd_in, bwd_in, gate_in, w_in = [
        local(src, dst, in_s.at[n]) for n, (src, dst) in enumerate(pairs)
    ]

    shares = [pl.ds(pl.multiple_of((x + d) % 4 * SHARE, SHARE), SHARE) for d in range(2)]

    def w_cols(n, high, cor, rows):
        at = (((z + ORDER[n]) % RING) * 4 + high * 2 + cor) * CHAN
        return w.at[rows, pl.ds(pl.multiple_of(at, CHAN), CHAN)]

    barrier = pltpu.get_barrier_semaphore()
    friends = [((i + d) % CTX, j) for d in range(1, CTX)]
    sibling = (i, z * 4 + hi * 2 + 1 - core)
    across = (i, z * 4 + (q + 2) % 4)
    friends += [sibling, across]
    friends += [(i, ((z + d) % RING) * 4 + q) for d in (1, RING - 1)]
    friends += [(x * 2 + 1 - lo, z * 4 + (1 - hi) * 2 + c) for c in range(2)]
    for friend in friends:
        pl.semaphore_signal(barrier, inc=1, device_id=friend, device_id_type=MESH)

    key_in.land()
    value_in.land()
    signal = key[...].astype(F32) * value[...].astype(F32)
    tsend[0] = signal.T.astype(BF16)
    filt_in.land()
    tsend[1] = filt[...].T.astype(BF16)
    pl.semaphore_wait(barrier, len(friends))

    def spread(t):
        copies = []
        for d in FARTHEST:
            to = (i + d) % CTX
            rows = pl.ds(pl.multiple_of(to * SUB, SUB), SUB)
            copies.append(remote(tsend.at[t, rows], trecv.at[t, i], t_ss.at[t, d - 1], t_rs.at[t, d - 1], (to, j)))
        rows = pl.ds(pl.multiple_of(i * SUB, SUB), SUB)
        copies.append(local(tsend.at[t, rows], trecv.at[t, i], loc_s.at[t]))
        return copies

    sig_copies = spread(0)
    fil_copies = spread(1)

    w_in.land()
    wy, wc = {}, []

    def along_y(first, last):
        for n in range(first, last):
            wy[n] = []
            for m in range(2):
                c = (core + m) % 2
                target = (x * 2 + 1 - lo, z * 4 + (1 - hi) * 2 + c)
                for d, rows in enumerate(shares if n in TWICE else shares[:1]):
                    src = w_cols(n, 1 - hi, c, rows)
                    wy[n].append(remote(src, wbuf.at[n, q, rows], wy_ss.at[n, m, d], wy_rs.at[n, m, d], target))

    along_y(0, RING)
    every = pl.ds(0, CHAN)
    wx = {}

    def along_x(g, first, last):
        for n in range(first, last):
            for copy in wy[n]:
                copy.land()
        if first in TWICE:
            plan = ((1, shares[0]), (3, shares[1]))
        else:
            plan = ((1, shares[0]), (3, shares[0]), (2, shares[0]))
        for d, rows in plan:
            block = wbuf.at[pl.ds(first, last - first), pl.ds((1 - hi) * 2, 2), rows]
            target = (((x + d) % 4) * 2 + lo, j)
            copy = remote(block, block, wx_ss.at[g, d - 1], wx_rs.at[g, d - 1], target)
            for n in range(first, last):
                wx.setdefault(n, []).append(copy)

    fwd_in.land()
    for copy in sig_copies:
        copy.land()
    for h in range(2):
        lhs = trecv[0, :, :, h * BLOCK : (h + 1) * BLOCK].reshape(CTX * SUB, BLOCK)
        sbuf[h] = dot(lhs, fwd[BLOCK:, :])
    for copy in fil_copies:
        copy.land()
    hbuf[1] = dot(trecv[1].reshape(CTX * SUB, POS), fwd[...])
    hbuf[0] = dot(trecv[1, :, :, :BLOCK].reshape(CTX * SUB, BLOCK), fwd[BLOCK:, :])
    hbuf[0, SUB:, :] += dot(trecv[1, : CTX - 1, :, BLOCK:].reshape((CTX - 1) * SUB, BLOCK), fwd[:BLOCK, :])

    along_x(0, 0, 1)
    bwd_in.land()
    mine_rows = pl.ds(pl.multiple_of(i * SUB, SUB), SUB)
    back = []
    for h in range(2):
        @pl.loop(0, (SUB // 8) * (BLOCK // 128))
        def _(t):
            row0 = (t // 2) * 8
            lane_re = pl.multiple_of((t % 2) * 128, 128)
            lane_im = pl.multiple_of(BLOCK + (t % 2) * 128, 128)

            def at(a):
                return pl.ds(pl.multiple_of((a // 2) * SUB + row0, 8), 8)

            def take(ref, a):
                return ref[a % 2, at(a), pl.ds(lane_re, 128)], ref[a % 2, at(a), pl.ds(lane_im, 128)]

            for a in range(h, BLOCKS, 2):
                re = im = None
                for d in range(a + 1):
                    sr, si = take(sbuf, a - d)
                    hr, hm = take(hbuf, d)
                    pr = sr * hr - si * hm
                    pm = sr * hm + si * hr
                    re = pr if re is None else re + pr
                    im = pm if im is None else im + pm
                zbuf[h, at(a), pl.ds(lane_re, 128)] = re
                zbuf[h, at(a), pl.ds(lane_im, 128)] = im

        csend[h] = dot(zbuf[h].astype(BF16), bwd[...]).astype(BF16)
        copies = []
        for d in FARTHEST:
            to = (i + d) % CTX
            rows = pl.ds(pl.multiple_of(to * SUB, SUB), SUB)
            copies.append(
                remote(csend.at[h, rows], crecv.at[h, mine_rows], c_ss.at[h, d - 1], c_rs.at[h, d - 1], (to, j))
            )
        if h == 0:
            along_x(1, 1, 3)
        copies.append(local(csend.at[h, mine_rows], crecv.at[h, mine_rows], loc_s.at[2 + h]))
        back.append(copies)

    for n in range(RING):
        wc.append(remote(w_cols(n, hi, 1 - core, every), wbuf.at[n, q], wc_ss.at[n], wc_rs.at[n], sibling))

    gate_in.land()
    cross, beside, passed = [], [], []
    for h in range(2):
        rows = pl.ds(h * BLOCK, BLOCK)
        for copy in back[h]:
            copy.land()
        convolved = crecv[h].astype(F32).T
        signal = key[rows, :].astype(F32) * value[rows, :].astype(F32)
        gall[q, rows] = ((convolved + skip[...] * signal) * gate[rows, :].astype(F32)).astype(BF16)
        for r in (2 * h, 2 * h + 1):
            block = gall.at[q, pl.ds(r * PIECE, PIECE)]
            cross.append(remote(block, block, g_ss.at[r, 0], g_rs.at[r, 0], across))
            beside.append(remote(block, block, g_ss.at[r, 1], g_rs.at[r, 1], sibling))
    along_x(2, 3, 5)
    along_x(3, 5, 8)

    def hand_on(r):
        cross[r].land()
        block = gall.at[(q + 2) % 4, pl.ds(r * PIECE, PIECE)]
        passed.append(remote(block, block, g_ss.at[r, 2], g_rs.at[r, 2], sibling))

    ready = set()

    def partial(far, first, count):
        n = ORDER.index(far)
        if n not in ready:
            ready.add(n)
            for copy in [wc[n]] + wx[n]:
                if not copy.landed:
                    copy.land()
        rows = pl.ds(first, count)
        total = dot(gall[q, rows], w_cols(n, hi, core, every)[...])
        for k in range(1, 4):
            at = (q + k) % 4
            total += dot(gall[at, rows], wbuf[n, at])
        pbuf[n, rows] = total

    turns = []
    for way in range(2):
        near, far = (way, 2 + way), (1 - way, 3 - way)
        turn = [((r + way) % 2, r) for r in range(4)] + [(1, r) for r in near]
        for step in (2, 3):
            turn += [(step, r) for r in far + near]
        turns.append(turn)
    sums = {}
    ahead = {4: (2,), 6: (6,), 8: (1,), 10: (7,), 12: (0,)}
    for n in range(len(turns[0])):
        if n == 0:
            hand_on(0)
        if n < 4:
            beside[n].land()
            passed[n].land()
        for far in ahead.get(n, ()):
            partial(far, 0, POS)
        for way, near in ((0, 1), (1, RING - 1)):
            step, r = turns[way][n]
            far = 4 - step if way == 0 else 4 + step
            if n < 6:
                partial(far, r * PIECE, PIECE)
            if way == 1 and n < 3:
                hand_on(n + 1)
            rows = pl.ds(r * PIECE, PIECE)
            total = pbuf[ORDER.index(far), rows]
            if (way, step - 1, r) in sums:
                sums[way, step - 1, r].land()
                total = total + rrecv[way, step - 1, rows].astype(F32)
            rsend[way, step, rows] = total.astype(BF16)
            sums[way, step, r] = remote(
                rsend.at[way, step, rows],
                rrecv.at[way, step, rows],
                r_ss.at[way, step, r],
                r_rs.at[way, step, r],
                (i, ((z + near) % RING) * 4 + q),
            )
    for r in (1, 3, 0, 2):
        rows = pl.ds(r * PIECE, PIECE)
        total = pbuf[ORDER.index(0), rows]
        for way in range(2):
            sums[way, 3, r].land()
            total = total + rrecv[way, 3, rows].astype(F32)
        out[rows, :] = total.astype(BF16)

    for copy in log:
        copy.leave()


def body(gate, key, value, filt, skip, w, fwd, bwd):
    vmem = pl.BlockSpec(memory_space=pltpu.VMEM)
    hbm = pl.BlockSpec(memory_space=pltpu.HBM)
    dma = pltpu.SemaphoreType.DMA
    return pl.pallas_call(
        kernel,
        out_shape=jax.ShapeDtypeStruct((POS, CHAN), BF16),
        in_specs=[hbm] * 4 + [vmem] + [hbm] * 3,
        out_specs=vmem,
        scratch_shapes=[
            pltpu.VMEM((POS, CHAN), BF16),
            pltpu.VMEM((POS, CHAN), BF16),
            pltpu.VMEM((POS, CHAN), BF16),
            pltpu.VMEM((POS, CHAN), F32),
            pltpu.VMEM((2 * BLOCK, 2 * BLOCK), BF16),
            pltpu.VMEM((2 * BLOCK, BLOCK), BF16),
            pltpu.VMEM((CHAN, RING * 4 * CHAN), BF16),
            pltpu.VMEM((2, CHAN, POS), BF16),
            pltpu.VMEM((2, CTX, SUB, POS), BF16),
            pltpu.VMEM((2, CHAN, 2 * BLOCK), F32),
            pltpu.VMEM((2, CHAN, 2 * BLOCK), F32),
            pltpu.VMEM((2, CHAN, 2 * BLOCK), F32),
            pltpu.VMEM((2, CHAN, BLOCK), BF16),
            pltpu.VMEM((2, CHAN, BLOCK), BF16),
            pltpu.VMEM((4, POS, CHAN), BF16),
            pltpu.VMEM((RING, 4, CHAN, CHAN), BF16),
            pltpu.VMEM((RING, POS, CHAN), F32),
            pltpu.VMEM((2, 4, POS, CHAN), BF16),
            pltpu.VMEM((2, 4, POS, CHAN), BF16),
            dma((2, CTX - 1)),
            dma((2, CTX - 1)),
            dma((2, CTX - 1)),
            dma((2, CTX - 1)),
            dma((4, 3)),
            dma((4, 3)),
            dma((RING,)),
            dma((RING,)),
            dma((RING, 2, 2)),
            dma((RING, 2, 2)),
            dma((4, 3)),
            dma((4, 3)),
            dma((2, 4, POS // PIECE)),
            dma((2, 4, POS // PIECE)),
            dma((4,)),
            dma((7,)),
        ],
        compiler_params=pltpu.CompilerParams(
            collective_id=0, has_side_effects=True, vmem_limit_bytes=64 * 1024 * 1024
        ),
        name="hyena",
    )(gate, key, value, filt, skip.reshape(1, CHAN), w, fwd, bwd)


def solution(mesh):
    mapped = jax.shard_map(
        body,
        mesh=mesh,
        in_specs=(P("ctx", "ch"),) * 4 + (P("ch"), P("ch", None), P(), P()),
        out_specs=P("ctx", "ch"),
        check_vma=False,
    )

    def run(out_gate, key_proj, value_proj, filters, skip_gain, out_weight):
        return mapped(out_gate, key_proj, value_proj, filters, skip_gain, out_weight, *tables())

    return run
```

```python
import functools

import jax
import jax.numpy as jnp
import numpy as np
from jax import lax
from jax.experimental import pallas as pl
from jax.experimental.pallas import tpu as pltpu
from jax.sharding import PartitionSpec as P

MESH = pl.DeviceIdType.MESH
F32 = jnp.float32
BF16 = jnp.bfloat16

CTX = 8
POS = 512
CHAN = 256
FARTHEST = (4, 5, 3, 2, 6, 1, 7)
SUB = CHAN // CTX
BLOCK = 256
BLOCKS = 16
PIECE = 128
RING = 8
ORDER = (4, 3, 5, 2, 6, 1, 7, 0)
SHARE = CHAN // 4
TWICE = (1, 2)


def dot(a, b):
    return jnp.dot(a, b, preferred_element_type=F32)


class Move:
    def __init__(self, copy, log):
        self.copy, self.landed, self.remote = copy, False, copy.is_remote
        copy.start()
        log.append(self)

    def land(self):
        self.landed = True
        if self.remote:
            self.copy.wait_recv()
        else:
            self.copy.wait()

    def leave(self):
        if self.remote:
            self.copy.wait_send()


def tables():
    theta = np.pi * (2 * np.arange(BLOCK) + 1) / (2 * BLOCK)
    at = np.arange(-BLOCK, BLOCK)[:, None] * theta[None, :]
    forward = np.concatenate((np.cos(at), -np.sin(at)), axis=1)
    back_at = theta[:, None] * np.arange(BLOCK)[None, :]
    backward = np.concatenate((np.cos(back_at), -np.sin(back_at)), axis=0) / BLOCK
    return jnp.asarray(forward, BF16), jnp.asarray(backward, BF16)


def kernel(
    gate_h,
    key_h,
    value_h,
    filt_h,
    skip,
    w_h,
    fwd_h,
    bwd_h,
    out,
    gate,
    key,
    value,
    filt,
    fwd,
    bwd,
    w,
    tsend,
    trecv,
    sbuf,
    hbuf,
    zbuf,
    csend,
    crecv,
    gall,
    wbuf,
    pbuf,
    rsend,
    rrecv,
    t_ss,
    t_rs,
    c_ss,
    c_rs,
    g_ss,
    g_rs,
    wc_ss,
    wc_rs,
    wy_ss,
    wy_rs,
    wx_ss,
    wx_rs,
    r_ss,
    r_rs,
    loc_s,
    in_s,
):
    log = []
    i = lax.axis_index("ctx")
    j = lax.axis_index("ch")
    x, lo = i // 2, i % 2
    z, q = j // 4, j % 4
    hi, core = q // 2, q % 2

    def remote(src, dst, ss, rs, device):
        copy = pltpu.make_async_remote_copy(
            src_ref=src, dst_ref=dst, send_sem=ss, recv_sem=rs, device_id=device, device_id_type=MESH
        )
        return Move(copy, log)

    def local(src, dst, sem):
        return Move(pltpu.make_async_copy(src, dst, sem), log)

    pairs = ((key_h, key), (value_h, value), (filt_h, filt), (fwd_h, fwd), (bwd_h, bwd), (gate_h, gate), (w_h, w))
    key_in, value_in, filt_in, fwd_in, bwd_in, gate_in, w_in = [
        local(src, dst, in_s.at[n]) for n, (src, dst) in enumerate(pairs)
    ]

    shares = [pl.ds(pl.multiple_of((x + d) % 4 * SHARE, SHARE), SHARE) for d in range(2)]

    def w_cols(n, high, cor, rows):
        at = (((z + ORDER[n]) % RING) * 4 + high * 2 + cor) * CHAN
        return w.at[rows, pl.ds(pl.multiple_of(at, CHAN), CHAN)]

    barrier = pltpu.get_barrier_semaphore()
    friends = [((i + d) % CTX, j) for d in range(1, CTX)]
    sibling = (i, z * 4 + hi * 2 + 1 - core)
    across = (i, z * 4 + (q + 2) % 4)
    friends += [sibling, across]
    friends += [(i, ((z + d) % RING) * 4 + q) for d in (1, RING - 1)]
    friends += [(x * 2 + 1 - lo, z * 4 + (1 - hi) * 2 + c) for c in range(2)]
    for friend in friends:
        pl.semaphore_signal(barrier, inc=1, device_id=friend, device_id_type=MESH)

    key_in.land()
    value_in.land()
    signal = key[...].astype(F32) * value[...].astype(F32)
    tsend[0] = signal.T.astype(BF16)
    filt_in.land()
    tsend[1] = filt[...].T.astype(BF16)
    pl.semaphore_wait(barrier, len(friends))

    def spread(t):
        copies = []
        for d in FARTHEST:
            to = (i + d) % CTX
            rows = pl.ds(pl.multiple_of(to * SUB, SUB), SUB)
            copies.append(remote(tsend.at[t, rows], trecv.at[t, i], t_ss.at[t, d - 1], t_rs.at[t, d - 1], (to, j)))
        rows = pl.ds(pl.multiple_of(i * SUB, SUB), SUB)
        copies.append(local(tsend.at[t, rows], trecv.at[t, i], loc_s.at[t]))
        return copies

    sig_copies = spread(0)
    fil_copies = spread(1)

    w_in.land()
    wy, wc = {}, []

    def along_y(first, last):
        for n in range(first, last):
            wy[n] = []
            for m in range(2):
                c = (core + m) % 2
                target = (x * 2 + 1 - lo, z * 4 + (1 - hi) * 2 + c)
                for d, rows in enumerate(shares if n in TWICE else shares[:1]):
                    src = w_cols(n, 1 - hi, c, rows)
                    wy[n].append(remote(src, wbuf.at[n, q, rows], wy_ss.at[n, m, d], wy_rs.at[n, m, d], target))

    along_y(0, RING)
    every = pl.ds(0, CHAN)
    wx = {}

    def along_x(g, first, last):
        for n in range(first, last):
            for copy in wy[n]:
                copy.land()
        if first in TWICE:
            plan = ((1, shares[0]), (3, shares[1]))
        else:
            plan = ((1, shares[0]), (3, shares[0]), (2, shares[0]))
        for d, rows in plan:
            block = wbuf.at[pl.ds(first, last - first), pl.ds((1 - hi) * 2, 2), rows]
            target = (((x + d) % 4) * 2 + lo, j)
            copy = remote(block, block, wx_ss.at[g, d - 1], wx_rs.at[g, d - 1], target)
            for n in range(first, last):
                wx.setdefault(n, []).append(copy)

    fwd_in.land()
    for copy in sig_copies:
        copy.land()
    for h in range(2):
        lhs = trecv[0, :, :, h * BLOCK : (h + 1) * BLOCK].reshape(CTX * SUB, BLOCK)
        sbuf[h] = dot(lhs, fwd[BLOCK:, :])
    for copy in fil_copies:
        copy.land()
    hbuf[1] = dot(trecv[1].reshape(CTX * SUB, POS), fwd[...])
    hbuf[0] = dot(trecv[1, :, :, :BLOCK].reshape(CTX * SUB, BLOCK), fwd[BLOCK:, :])
    hbuf[0, SUB:, :] += dot(trecv[1, : CTX - 1, :, BLOCK:].reshape((CTX - 1) * SUB, BLOCK), fwd[:BLOCK, :])

    along_x(0, 0, 1)
    gate_in.land()
    pbuf[0] = skip[...] * (key[...].astype(F32) * value[...].astype(F32)) * gate[...].astype(F32)
    bwd_in.land()
    mine_rows = pl.ds(pl.multiple_of(i * SUB, SUB), SUB)
    back = []
    for h in range(2):
        @pl.loop(0, (SUB // 8) * (BLOCK // 128))
        def _(t):
            row0 = (t // 2) * 8
            lane_re = pl.multiple_of((t % 2) * 128, 128)
            lane_im = pl.multiple_of(BLOCK + (t % 2) * 128, 128)

            def at(a):
                return pl.ds(pl.multiple_of((a // 2) * SUB + row0, 8), 8)

            def take(ref, a):
                return ref[a % 2, at(a), pl.ds(lane_re, 128)], ref[a % 2, at(a), pl.ds(lane_im, 128)]

            for a in range(h, BLOCKS, 2):
                re = im = None
                for d in range(a + 1):
                    sr, si = take(sbuf, a - d)
                    hr, hm = take(hbuf, d)
                    pr = sr * hr - si * hm
                    pm = sr * hm + si * hr
                    re = pr if re is None else re + pr
                    im = pm if im is None else im + pm
                zbuf[h, at(a), pl.ds(lane_re, 128)] = re
                zbuf[h, at(a), pl.ds(lane_im, 128)] = im

        csend[h] = dot(zbuf[h].astype(BF16), bwd[...]).astype(BF16)
        copies = []
        for d in FARTHEST:
            to = (i + d) % CTX
            rows = pl.ds(pl.multiple_of(to * SUB, SUB), SUB)
            copies.append(
                remote(csend.at[h, rows], crecv.at[h, mine_rows], c_ss.at[h, d - 1], c_rs.at[h, d - 1], (to, j))
            )
        if h == 0:
            along_x(1, 1, 3)
        copies.append(local(csend.at[h, mine_rows], crecv.at[h, mine_rows], loc_s.at[2 + h]))
        back.append(copies)

    for n in range(RING):
        wc.append(remote(w_cols(n, hi, 1 - core, every), wbuf.at[n, q], wc_ss.at[n], wc_rs.at[n], sibling))

    cross, beside, passed = [], [], []
    for h in range(2):
        rows = pl.ds(h * BLOCK, BLOCK)
        for copy in back[h]:
            copy.land()
        if h == 1:
            along_x(2, 3, 5)
        convolved = crecv[h].astype(F32).T
        gall[q, rows] = (convolved * gate[rows, :].astype(F32) + pbuf[0, rows]).astype(BF16)
        for r in (2 * h, 2 * h + 1):
            block = gall.at[q, pl.ds(r * PIECE, PIECE)]
            cross.append(remote(block, block, g_ss.at[r, 0], g_rs.at[r, 0], across))
            beside.append(remote(block, block, g_ss.at[r, 1], g_rs.at[r, 1], sibling))
    along_x(3, 5, 8)

    def hand_on(r):
        cross[r].land()
        block = gall.at[(q + 2) % 4, pl.ds(r * PIECE, PIECE)]
        passed.append(remote(block, block, g_ss.at[r, 2], g_rs.at[r, 2], sibling))

    ready = set()

    def partial(far, first, count):
        n = ORDER.index(far)
        if n not in ready:
            ready.add(n)
            for copy in [wc[n]] + wx[n]:
                if not copy.landed:
                    copy.land()
        rows = pl.ds(first, count)
        total = dot(gall[q, rows], w_cols(n, hi, core, every)[...])
        for k in range(1, 4):
            at = (q + k) % 4
            total += dot(gall[at, rows], wbuf[n, at])
        pbuf[n, rows] = total

    turns = []
    for way in range(2):
        near, far = (way, 2 + way), (1 - way, 3 - way)
        turn = [((r + way) % 2, r) for r in range(4)] + [(1, r) for r in near]
        for step in (2, 3):
            turn += [(step, r) for r in far + near]
        turns.append(turn)
    sums = {}
    ahead = {6: (2, 6), 10: (1, 7), 13: (0,)}
    for n in range(len(turns[0])):
        if n == 0:
            hand_on(0)
        if n < 4:
            beside[n].land()
            passed[n].land()
        for far in ahead.get(n, ()):
            partial(far, 0, POS)
        for way, near in ((0, 1), (1, RING - 1)):
            step, r = turns[way][n]
            far = 4 - step if way == 0 else 4 + step
            if n < 6:
                partial(far, r * PIECE, PIECE)
            if way == 1 and n < 3:
                hand_on(n + 1)
            rows = pl.ds(r * PIECE, PIECE)
            total = pbuf[ORDER.index(far), rows]
            if (way, step - 1, r) in sums:
                sums[way, step - 1, r].land()
                total = total + rrecv[way, step - 1, rows].astype(F32)
            rsend[way, step, rows] = total.astype(BF16)
            sums[way, step, r] = remote(
                rsend.at[way, step, rows],
                rrecv.at[way, step, rows],
                r_ss.at[way, step, r],
                r_rs.at[way, step, r],
                (i, ((z + near) % RING) * 4 + q),
            )
    for r in (1, 3, 0, 2):
        rows = pl.ds(r * PIECE, PIECE)
        total = pbuf[ORDER.index(0), rows]
        for way in range(2):
            sums[way, 3, r].land()
            total = total + rrecv[way, 3, rows].astype(F32)
        out[rows, :] = total.astype(BF16)

    for copy in log:
        copy.leave()


def body(gate, key, value, filt, skip, w, fwd, bwd):
    vmem = pl.BlockSpec(memory_space=pltpu.VMEM)
    hbm = pl.BlockSpec(memory_space=pltpu.HBM)
    dma = pltpu.SemaphoreType.DMA
    return pl.pallas_call(
        kernel,
        out_shape=pltpu.VMEM((POS, CHAN), BF16),
        in_specs=[hbm] * 4 + [vmem] + [hbm] * 3,
        out_specs=vmem,
        scratch_shapes=[
            pltpu.VMEM((POS, CHAN), BF16),
            pltpu.VMEM((POS, CHAN), BF16),
            pltpu.VMEM((POS, CHAN), BF16),
            pltpu.VMEM((POS, CHAN), F32),
            pltpu.VMEM((2 * BLOCK, 2 * BLOCK), BF16),
            pltpu.VMEM((2 * BLOCK, BLOCK), BF16),
            pltpu.VMEM((CHAN, RING * 4 * CHAN), BF16),
            pltpu.VMEM((2, CHAN, POS), BF16),
            pltpu.VMEM((2, CTX, SUB, POS), BF16),
            pltpu.VMEM((2, CHAN, 2 * BLOCK), F32),
            pltpu.VMEM((2, CHAN, 2 * BLOCK), F32),
            pltpu.VMEM((2, CHAN, 2 * BLOCK), F32),
            pltpu.VMEM((2, CHAN, BLOCK), BF16),
            pltpu.VMEM((2, CHAN, BLOCK), BF16),
            pltpu.VMEM((4, POS, CHAN), BF16),
            pltpu.VMEM((RING, 4, CHAN, CHAN), BF16),
            pltpu.VMEM((RING, POS, CHAN), F32),
            pltpu.VMEM((2, 4, POS, CHAN), BF16),
            pltpu.VMEM((2, 4, POS, CHAN), BF16),
            dma((2, CTX - 1)),
            dma((2, CTX - 1)),
            dma((2, CTX - 1)),
            dma((2, CTX - 1)),
            dma((4, 3)),
            dma((4, 3)),
            dma((RING,)),
            dma((RING,)),
            dma((RING, 2, 2)),
            dma((RING, 2, 2)),
            dma((4, 3)),
            dma((4, 3)),
            dma((2, 4, POS // PIECE)),
            dma((2, 4, POS // PIECE)),
            dma((4,)),
            dma((7,)),
        ],
        compiler_params=pltpu.CompilerParams(
            collective_id=0, has_side_effects=True, vmem_limit_bytes=64 * 1024 * 1024 - 1024 * 1024
        ),
        name="hyena",
    )(gate, key, value, filt, skip.reshape(1, CHAN), w, fwd, bwd)


def solution(mesh):
    mapped = jax.shard_map(
        body,
        mesh=mesh,
        in_specs=(P("ctx", "ch"),) * 4 + (P("ch"), P("ch", None), P(), P()),
        out_specs=P("ctx", "ch"),
        check_vma=False,
    )

    def run(out_gate, key_proj, value_proj, filters, skip_gain, out_weight):
        return mapped(out_gate, key_proj, value_proj, filters, skip_gain, out_weight, *tables())

    return run
```

```python
import functools

import jax
import jax.numpy as jnp
import numpy as np
from jax import lax
from jax.experimental import pallas as pl
from jax.experimental.pallas import tpu as pltpu
from jax.sharding import PartitionSpec as P

MESH = pl.DeviceIdType.MESH
F32 = jnp.float32
BF16 = jnp.bfloat16

CTX = 8
POS = 512
CHAN = 256
FARTHEST = (4, 5, 3, 2, 6, 1, 7)
SUB = CHAN // CTX
BLOCK = 256
BLOCKS = 16
PIECE = 128
RING = 8
ORDER = (4, 3, 5, 2, 6, 1, 7, 0)
SHARE = CHAN // 4
TWICE = (1, 2)


def dot(a, b):
    return jnp.dot(a, b, preferred_element_type=F32)


class Move:
    def __init__(self, copy, log):
        self.copy, self.landed, self.remote = copy, False, copy.is_remote
        copy.start()
        log.append(self)

    def land(self):
        self.landed = True
        if self.remote:
            self.copy.wait_recv()
        else:
            self.copy.wait()

    def leave(self):
        if self.remote:
            self.copy.wait_send()


def tables():
    theta = np.pi * (2 * np.arange(BLOCK) + 1) / (2 * BLOCK)
    at = np.arange(-BLOCK, BLOCK)[:, None] * theta[None, :]
    forward = np.concatenate((np.cos(at), -np.sin(at)), axis=1)
    back_at = theta[:, None] * np.arange(BLOCK)[None, :]
    backward = np.concatenate((np.cos(back_at), -np.sin(back_at)), axis=0) / BLOCK
    return jnp.asarray(forward, BF16), jnp.asarray(backward, BF16)


def kernel(
    gate_h,
    key_h,
    value_h,
    filt_h,
    skip,
    w_h,
    fwd_h,
    bwd_h,
    out,
    gate,
    key,
    value,
    filt,
    fwd,
    bwd,
    w,
    tsend,
    trecv,
    sbuf,
    hbuf,
    zbuf,
    csend,
    crecv,
    gall,
    wbuf,
    pbuf,
    rsend,
    rrecv,
    t_ss,
    t_rs,
    c_ss,
    c_rs,
    g_ss,
    g_rs,
    wc_ss,
    wc_rs,
    wy_ss,
    wy_rs,
    wx_ss,
    wx_rs,
    r_ss,
    r_rs,
    loc_s,
    in_s,
):
    log = []
    i = lax.axis_index("ctx")
    j = lax.axis_index("ch")
    x, lo = i // 2, i % 2
    z, q = j // 4, j % 4
    hi, core = q // 2, q % 2

    def remote(src, dst, ss, rs, device):
        copy = pltpu.make_async_remote_copy(
            src_ref=src, dst_ref=dst, send_sem=ss, recv_sem=rs, device_id=device, device_id_type=MESH
        )
        return Move(copy, log)

    def local(src, dst, sem):
        return Move(pltpu.make_async_copy(src, dst, sem), log)

    pairs = ((key_h, key), (value_h, value), (filt_h, filt), (fwd_h, fwd), (bwd_h, bwd), (gate_h, gate), (w_h, w))
    key_in, value_in, filt_in, fwd_in, bwd_in, gate_in, w_in = [
        local(src, dst, in_s.at[n]) for n, (src, dst) in enumerate(pairs)
    ]

    shares = [pl.ds(pl.multiple_of((x + d) % 4 * SHARE, SHARE), SHARE) for d in range(2)]

    def w_cols(n, high, cor, rows):
        at = (((z + ORDER[n]) % RING) * 4 + high * 2 + cor) * CHAN
        return w.at[rows, pl.ds(pl.multiple_of(at, CHAN), CHAN)]

    barrier = pltpu.get_barrier_semaphore()
    friends = [((i + d) % CTX, j) for d in range(1, CTX)]
    sibling = (i, z * 4 + hi * 2 + 1 - core)
    across = (i, z * 4 + (q + 2) % 4)
    friends += [sibling, across]
    friends += [(i, ((z + d) % RING) * 4 + q) for d in (1, RING - 1)]
    friends += [(x * 2 + 1 - lo, z * 4 + (1 - hi) * 2 + c) for c in range(2)]
    for friend in friends:
        pl.semaphore_signal(barrier, inc=1, device_id=friend, device_id_type=MESH)

    key_in.land()
    value_in.land()
    signal = key[...].astype(F32) * value[...].astype(F32)
    tsend[0] = signal.T.astype(BF16)
    filt_in.land()
    tsend[1] = filt[...].T.astype(BF16)
    pl.semaphore_wait(barrier, len(friends))

    def spread(t):
        copies = []
        for d in FARTHEST:
            to = (i + d) % CTX
            rows = pl.ds(pl.multiple_of(to * SUB, SUB), SUB)
            copies.append(remote(tsend.at[t, rows], trecv.at[t, i], t_ss.at[t, d - 1], t_rs.at[t, d - 1], (to, j)))
        rows = pl.ds(pl.multiple_of(i * SUB, SUB), SUB)
        copies.append(local(tsend.at[t, rows], trecv.at[t, i], loc_s.at[t]))
        return copies

    fil_copies = spread(1)
    sig_copies = spread(0)

    w_in.land()
    wy, wc = {}, []

    def along_y(first, last):
        for n in range(first, last):
            wy[n] = []
            for m in range(2):
                c = (core + m) % 2
                target = (x * 2 + 1 - lo, z * 4 + (1 - hi) * 2 + c)
                for d, rows in enumerate(shares if n in TWICE else shares[:1]):
                    src = w_cols(n, 1 - hi, c, rows)
                    wy[n].append(remote(src, wbuf.at[n, q, rows], wy_ss.at[n, m, d], wy_rs.at[n, m, d], target))

    along_y(0, RING)
    every = pl.ds(0, CHAN)
    wx = {}

    def along_x(g, first, last):
        for n in range(first, last):
            for copy in wy[n]:
                copy.land()
        if first in TWICE:
            plan = ((1, shares[0]), (3, shares[1]))
        else:
            plan = ((1, shares[0]), (3, shares[0]), (2, shares[0]))
        for d, rows in plan:
            block = wbuf.at[pl.ds(first, last - first), pl.ds((1 - hi) * 2, 2), rows]
            target = (((x + d) % 4) * 2 + lo, j)
            copy = remote(block, block, wx_ss.at[g, d - 1], wx_rs.at[g, d - 1], target)
            for n in range(first, last):
                wx.setdefault(n, []).append(copy)

    gate_in.land()
    pbuf[0] = skip[...] * (key[...].astype(F32) * value[...].astype(F32)) * gate[...].astype(F32)

    fwd_in.land()
    for copy in fil_copies:
        copy.land()
    hbuf[1] = dot(trecv[1].reshape(CTX * SUB, POS), fwd[...])
    hbuf[0] = dot(trecv[1, :, :, :BLOCK].reshape(CTX * SUB, BLOCK), fwd[BLOCK:, :])
    hbuf[0, SUB:, :] += dot(trecv[1, : CTX - 1, :, BLOCK:].reshape((CTX - 1) * SUB, BLOCK), fwd[:BLOCK, :])

    for copy in sig_copies:
        copy.land()
    for h in range(2):
        lhs = trecv[0, :, :, h * BLOCK : (h + 1) * BLOCK].reshape(CTX * SUB, BLOCK)
        sbuf[h] = dot(lhs, fwd[BLOCK:, :])
    along_x(0, 0, 1)
    bwd_in.land()
    mine_rows = pl.ds(pl.multiple_of(i * SUB, SUB), SUB)
    back = []
    for h in range(2):
        @pl.loop(0, (SUB // 8) * (BLOCK // 128))
        def _(t):
            row0 = (t // 2) * 8
            lane_re = pl.multiple_of((t % 2) * 128, 128)
            lane_im = pl.multiple_of(BLOCK + (t % 2) * 128, 128)

            def at(a):
                return pl.ds(pl.multiple_of((a // 2) * SUB + row0, 8), 8)

            def take(ref, a):
                return ref[a % 2, at(a), pl.ds(lane_re, 128)], ref[a % 2, at(a), pl.ds(lane_im, 128)]

            for a in range(h, BLOCKS, 2):
                re = im = None
                for d in range(a + 1):
                    sr, si = take(sbuf, a - d)
                    hr, hm = take(hbuf, d)
                    pr = sr * hr - si * hm
                    pm = sr * hm + si * hr
                    re = pr if re is None else re + pr
                    im = pm if im is None else im + pm
                zbuf[h, at(a), pl.ds(lane_re, 128)] = re
                zbuf[h, at(a), pl.ds(lane_im, 128)] = im

        csend[h] = dot(zbuf[h].astype(BF16), bwd[...]).astype(BF16)
        copies = []
        for d in FARTHEST:
            to = (i + d) % CTX
            rows = pl.ds(pl.multiple_of(to * SUB, SUB), SUB)
            copies.append(
                remote(csend.at[h, rows], crecv.at[h, mine_rows], c_ss.at[h, d - 1], c_rs.at[h, d - 1], (to, j))
            )
        if h == 0:
            along_x(1, 1, 3)
        copies.append(local(csend.at[h, mine_rows], crecv.at[h, mine_rows], loc_s.at[2 + h]))
        back.append(copies)

    for n in range(RING):
        wc.append(remote(w_cols(n, hi, 1 - core, every), wbuf.at[n, q], wc_ss.at[n], wc_rs.at[n], sibling))

    cross, beside, passed = [], [], []
    for h in range(2):
        for copy in back[h]:
            copy.land()
        if h == 1:
            along_x(2, 3, 5)
        for r in (2 * h, 2 * h + 1):
            rows = pl.ds(r * PIECE, PIECE)
            convolved = crecv[h, :, pl.ds(r % 2 * PIECE, PIECE)].astype(F32).T
            gall[q, rows] = (convolved * gate[rows, :].astype(F32) + pbuf[0, rows]).astype(BF16)
            block = gall.at[q, rows]
            cross.append(remote(block, block, g_ss.at[r, 0], g_rs.at[r, 0], across))
            beside.append(remote(block, block, g_ss.at[r, 1], g_rs.at[r, 1], sibling))
    along_x(3, 5, 7)
    along_x(4, 7, 8)

    def hand_on(r):
        cross[r].land()
        block = gall.at[(q + 2) % 4, pl.ds(r * PIECE, PIECE)]
        passed.append(remote(block, block, g_ss.at[r, 2], g_rs.at[r, 2], sibling))

    ready = set()

    def partial(far, first, count):
        n = ORDER.index(far)
        if n not in ready:
            ready.add(n)
            for copy in [wc[n]] + wx[n]:
                if not copy.landed:
                    copy.land()
        rows = pl.ds(first, count)
        total = dot(gall[q, rows], w_cols(n, hi, core, every)[...])
        for k in range(1, 4):
            at = (q + k) % 4
            total += dot(gall[at, rows], wbuf[n, at])
        pbuf[n, rows] = total

    turns = []
    for way in range(2):
        near, far = (way, 2 + way), (1 - way, 3 - way)
        turn = [((r + way) % 2, r) for r in range(4)] + [(1, r) for r in near]
        for step in (2, 3):
            turn += [(step, r) for r in far + near]
        turns.append(turn)
    sums = {}
    ahead = {6: (2, 6), 10: (1, 7), 13: (0,)}
    for n in range(len(turns[0])):
        if n == 0:
            hand_on(0)
        if n < 4:
            beside[n].land()
            passed[n].land()
        for far in ahead.get(n, ()):
            partial(far, 0, POS)
        for way, near in ((0, 1), (1, RING - 1)):
            step, r = turns[way][n]
            far = 4 - step if way == 0 else 4 + step
            if n < 6:
                partial(far, r * PIECE, PIECE)
            if way == 1 and n < 3:
                hand_on(n + 1)
            rows = pl.ds(r * PIECE, PIECE)
            total = pbuf[ORDER.index(far), rows]
            if (way, step - 1, r) in sums:
                sums[way, step - 1, r].land()
                total = total + rrecv[way, step - 1, rows].astype(F32)
            rsend[way, step, rows] = total.astype(BF16)
            sums[way, step, r] = remote(
                rsend.at[way, step, rows],
                rrecv.at[way, step, rows],
                r_ss.at[way, step, r],
                r_rs.at[way, step, r],
                (i, ((z + near) % RING) * 4 + q),
            )
    for r in (1, 3, 0, 2):
        rows = pl.ds(r * PIECE, PIECE)
        total = pbuf[ORDER.index(0), rows]
        for way in range(2):
            sums[way, 3, r].land()
            total = total + rrecv[way, 3, rows].astype(F32)
        out[rows, :] = total.astype(BF16)

    for copy in log:
        copy.leave()


def body(gate, key, value, filt, skip, w, fwd, bwd):
    vmem = pl.BlockSpec(memory_space=pltpu.VMEM)
    hbm = pl.BlockSpec(memory_space=pltpu.HBM)
    dma = pltpu.SemaphoreType.DMA
    return pl.pallas_call(
        kernel,
        out_shape=pltpu.VMEM((POS, CHAN), BF16),
        in_specs=[hbm] * 4 + [vmem] + [hbm] * 3,
        out_specs=vmem,
        scratch_shapes=[
            pltpu.VMEM((POS, CHAN), BF16),
            pltpu.VMEM((POS, CHAN), BF16),
            pltpu.VMEM((POS, CHAN), BF16),
            pltpu.VMEM((POS, CHAN), F32),
            pltpu.VMEM((2 * BLOCK, 2 * BLOCK), BF16),
            pltpu.VMEM((2 * BLOCK, BLOCK), BF16),
            pltpu.VMEM((CHAN, RING * 4 * CHAN), BF16),
            pltpu.VMEM((2, CHAN, POS), BF16),
            pltpu.VMEM((2, CTX, SUB, POS), BF16),
            pltpu.VMEM((2, CHAN, 2 * BLOCK), F32),
            pltpu.VMEM((2, CHAN, 2 * BLOCK), F32),
            pltpu.VMEM((2, CHAN, 2 * BLOCK), F32),
            pltpu.VMEM((2, CHAN, BLOCK), BF16),
            pltpu.VMEM((2, CHAN, BLOCK), BF16),
            pltpu.VMEM((4, POS, CHAN), BF16),
            pltpu.VMEM((RING, 4, CHAN, CHAN), BF16),
            pltpu.VMEM((RING, POS, CHAN), F32),
            pltpu.VMEM((2, 4, POS, CHAN), BF16),
            pltpu.VMEM((2, 4, POS, CHAN), BF16),
            dma((2, CTX - 1)),
            dma((2, CTX - 1)),
            dma((2, CTX - 1)),
            dma((2, CTX - 1)),
            dma((4, 3)),
            dma((4, 3)),
            dma((RING,)),
            dma((RING,)),
            dma((RING, 2, 2)),
            dma((RING, 2, 2)),
            dma((5, 3)),
            dma((5, 3)),
            dma((2, 4, POS // PIECE)),
            dma((2, 4, POS // PIECE)),
            dma((4,)),
            dma((7,)),
        ],
        compiler_params=pltpu.CompilerParams(
            collective_id=0, has_side_effects=True, vmem_limit_bytes=64 * 1024 * 1024 - 1024 * 1024
        ),
        name="hyena",
    )(gate, key, value, filt, skip.reshape(1, CHAN), w, fwd, bwd)


def solution(mesh):
    mapped = jax.shard_map(
        body,
        mesh=mesh,
        in_specs=(P("ctx", "ch"),) * 4 + (P("ch"), P("ch", None), P(), P()),
        out_specs=P("ctx", "ch"),
        check_vma=False,
    )

    def run(out_gate, key_proj, value_proj, filters, skip_gain, out_weight):
        return mapped(out_gate, key_proj, value_proj, filters, skip_gain, out_weight, *tables())

    return run
```

```python
import functools

import jax
import jax.numpy as jnp
import numpy as np
from jax import lax
from jax.experimental import pallas as pl
from jax.experimental.pallas import tpu as pltpu
from jax.sharding import PartitionSpec as P

MESH = pl.DeviceIdType.MESH
F32 = jnp.float32
BF16 = jnp.bfloat16

CTX = 8
POS = 512
CHAN = 256
FARTHEST = (4, 5, 3, 2, 6, 1, 7)
SUB = CHAN // CTX
BLOCK = 256
BLOCKS = 16
PIECE = 128
RING = 8
ORDER = (4, 3, 5, 2, 6, 1, 7, 0)
SHARE = CHAN // 4
TWICE = (1, 2)


def dot(a, b):
    return jnp.dot(a, b, preferred_element_type=F32)


class Move:
    def __init__(self, copy, log):
        self.copy, self.landed, self.remote = copy, False, copy.is_remote
        copy.start()
        log.append(self)

    def land(self):
        self.landed = True
        if self.remote:
            self.copy.wait_recv()
        else:
            self.copy.wait()

    def leave(self):
        if self.remote:
            self.copy.wait_send()


def tables():
    theta = np.pi * (2 * np.arange(BLOCK) + 1) / (2 * BLOCK)
    at = np.arange(-BLOCK, BLOCK)[:, None] * theta[None, :]
    forward = np.concatenate((np.cos(at), -np.sin(at)), axis=1)
    back_at = theta[:, None] * np.arange(BLOCK)[None, :]
    backward = np.concatenate((np.cos(back_at), -np.sin(back_at)), axis=0) / BLOCK
    return jnp.asarray(forward, BF16), jnp.asarray(backward, BF16)


def kernel(
    gate_h,
    key_h,
    value_h,
    filt_h,
    skip,
    w_h,
    fwd_h,
    bwd_h,
    out,
    gate,
    key,
    value,
    filt,
    fwd,
    bwd,
    w,
    tsend,
    trecv,
    sbuf,
    hbuf,
    zbuf,
    csend,
    crecv,
    gall,
    wbuf,
    pbuf,
    rsend,
    rrecv,
    t_ss,
    t_rs,
    c_ss,
    c_rs,
    g_ss,
    g_rs,
    wc_ss,
    wc_rs,
    wy_ss,
    wy_rs,
    wx_ss,
    wx_rs,
    r_ss,
    r_rs,
    loc_s,
    in_s,
):
    log = []
    i = lax.axis_index("ctx")
    j = lax.axis_index("ch")
    x, lo = i // 2, i % 2
    z, q = j // 4, j % 4
    hi, core = q // 2, q % 2

    def remote(src, dst, ss, rs, device):
        copy = pltpu.make_async_remote_copy(
            src_ref=src, dst_ref=dst, send_sem=ss, recv_sem=rs, device_id=device, device_id_type=MESH
        )
        return Move(copy, log)

    def local(src, dst, sem):
        return Move(pltpu.make_async_copy(src, dst, sem), log)

    pairs = ((key_h, key), (value_h, value), (filt_h, filt), (fwd_h, fwd), (bwd_h, bwd), (gate_h, gate), (w_h, w))
    key_in, value_in, filt_in, fwd_in, bwd_in, gate_in, w_in = [
        local(src, dst, in_s.at[n]) for n, (src, dst) in enumerate(pairs)
    ]

    shares = [pl.ds(pl.multiple_of((x + d) % 4 * SHARE, SHARE), SHARE) for d in range(2)]

    def w_cols(n, high, cor, rows):
        at = (((z + ORDER[n]) % RING) * 4 + high * 2 + cor) * CHAN
        return w.at[rows, pl.ds(pl.multiple_of(at, CHAN), CHAN)]

    barrier = pltpu.get_barrier_semaphore()
    friends = [((i + d) % CTX, j) for d in range(1, CTX)]
    sibling = (i, z * 4 + hi * 2 + 1 - core)
    across = (i, z * 4 + (q + 2) % 4)
    friends += [sibling, across]
    friends += [(i, ((z + d) % RING) * 4 + q) for d in (1, RING - 1)]
    friends += [(x * 2 + 1 - lo, z * 4 + (1 - hi) * 2 + c) for c in range(2)]
    for friend in friends:
        pl.semaphore_signal(barrier, inc=1, device_id=friend, device_id_type=MESH)

    key_in.land()
    value_in.land()
    signal = key[...].astype(F32) * value[...].astype(F32)
    tsend[0] = signal.T.astype(BF16)
    filt_in.land()
    tsend[1] = filt[...].T.astype(BF16)
    pl.semaphore_wait(barrier, len(friends))

    def spread(t):
        copies = []
        for d in FARTHEST:
            to = (i + d) % CTX
            rows = pl.ds(pl.multiple_of(to * SUB, SUB), SUB)
            copies.append(remote(tsend.at[t, rows], trecv.at[t, i], t_ss.at[t, d - 1], t_rs.at[t, d - 1], (to, j)))
        rows = pl.ds(pl.multiple_of(i * SUB, SUB), SUB)
        copies.append(local(tsend.at[t, rows], trecv.at[t, i], loc_s.at[t]))
        return copies

    fil_copies = spread(1)
    sig_copies = spread(0)

    w_in.land()
    wy, wc = {}, []

    def along_y(first, last):
        for n in range(first, last):
            wy[n] = []
            for m in range(2):
                c = (core + m) % 2
                target = (x * 2 + 1 - lo, z * 4 + (1 - hi) * 2 + c)
                for d, rows in enumerate(shares if n in TWICE else shares[:1]):
                    src = w_cols(n, 1 - hi, c, rows)
                    wy[n].append(remote(src, wbuf.at[n, q, rows], wy_ss.at[n, m, d], wy_rs.at[n, m, d], target))

    along_y(0, RING)
    every = pl.ds(0, CHAN)
    wx = {}

    def along_x(g, first, last):
        for n in range(first, last):
            for copy in wy[n]:
                copy.land()
        if first in TWICE:
            plan = ((1, shares[0]), (3, shares[1]))
        else:
            plan = ((1, shares[0]), (3, shares[0]), (2, shares[0]))
        for d, rows in plan:
            block = wbuf.at[pl.ds(first, last - first), pl.ds((1 - hi) * 2, 2), rows]
            target = (((x + d) % 4) * 2 + lo, j)
            copy = remote(block, block, wx_ss.at[g, d - 1], wx_rs.at[g, d - 1], target)
            for n in range(first, last):
                wx.setdefault(n, []).append(copy)

    gate_in.land()
    pbuf[0] = skip[...] * (key[...].astype(F32) * value[...].astype(F32)) * gate[...].astype(F32)

    fwd_in.land()
    for copy in fil_copies:
        copy.land()
    hbuf[1] = dot(trecv[1].reshape(CTX * SUB, POS), fwd[...])
    hbuf[0] = dot(trecv[1, :, :, :BLOCK].reshape(CTX * SUB, BLOCK), fwd[BLOCK:, :])
    hbuf[0, SUB:, :] += dot(trecv[1, : CTX - 1, :, BLOCK:].reshape((CTX - 1) * SUB, BLOCK), fwd[:BLOCK, :])

    for copy in sig_copies:
        copy.land()
    for h in range(2):
        lhs = trecv[0, :, :, h * BLOCK : (h + 1) * BLOCK].reshape(CTX * SUB, BLOCK)
        sbuf[h] = dot(lhs, fwd[BLOCK:, :])
    along_x(0, 0, 1)
    bwd_in.land()
    mine_rows = pl.ds(pl.multiple_of(i * SUB, SUB), SUB)
    back = []
    for h in range(2):
        @pl.loop(0, (SUB // 8) * (BLOCK // 128))
        def _(t):
            row0 = (t // 2) * 8
            lane_re = pl.multiple_of((t % 2) * 128, 128)
            lane_im = pl.multiple_of(BLOCK + (t % 2) * 128, 128)

            def at(a):
                return pl.ds(pl.multiple_of((a // 2) * SUB + row0, 8), 8)

            def take(ref, a):
                return ref[a % 2, at(a), pl.ds(lane_re, 128)], ref[a % 2, at(a), pl.ds(lane_im, 128)]

            for a in range(h, BLOCKS, 2):
                re = im = None
                for d in range(a + 1):
                    sr, si = take(sbuf, a - d)
                    hr, hm = take(hbuf, d)
                    pr = sr * hr - si * hm
                    pm = sr * hm + si * hr
                    re = pr if re is None else re + pr
                    im = pm if im is None else im + pm
                zbuf[h, at(a), pl.ds(lane_re, 128)] = re
                zbuf[h, at(a), pl.ds(lane_im, 128)] = im

        csend[h] = dot(zbuf[h].astype(BF16), bwd[...]).astype(BF16)
        copies = []
        for d in FARTHEST:
            to = (i + d) % CTX
            rows = pl.ds(pl.multiple_of(to * SUB, SUB), SUB)
            copies.append(
                remote(csend.at[h, rows], crecv.at[h, mine_rows], c_ss.at[h, d - 1], c_rs.at[h, d - 1], (to, j))
            )
        if h == 0:
            along_x(1, 1, 3)
        copies.append(local(csend.at[h, mine_rows], crecv.at[h, mine_rows], loc_s.at[2 + h]))
        back.append(copies)

    for n in range(RING):
        wc.append(remote(w_cols(n, hi, 1 - core, every), wbuf.at[n, q], wc_ss.at[n], wc_rs.at[n], sibling))

    cross, beside, passed = [], [], []
    for h in range(2):
        for copy in back[h]:
            copy.land()
        if h == 1:
            along_x(2, 3, 5)
        for r in (2 * h, 2 * h + 1):
            rows = pl.ds(r * PIECE, PIECE)
            convolved = crecv[h, :, pl.ds(r % 2 * PIECE, PIECE)].astype(F32).T
            gall[q, rows] = (convolved * gate[rows, :].astype(F32) + pbuf[0, rows]).astype(BF16)
            block = gall.at[q, rows]
            cross.append(remote(block, block, g_ss.at[r, 0], g_rs.at[r, 0], across))
            beside.append(remote(block, block, g_ss.at[r, 1], g_rs.at[r, 1], sibling))
    along_x(3, 5, 7)
    along_x(4, 7, 8)

    def hand_on(r):
        cross[r].land()
        block = gall.at[(q + 2) % 4, pl.ds(r * PIECE, PIECE)]
        passed.append(remote(block, block, g_ss.at[r, 2], g_rs.at[r, 2], sibling))

    ready = set()

    def partial(far, first, count):
        n = ORDER.index(far)
        if n not in ready:
            ready.add(n)
            for copy in [wc[n]] + wx[n]:
                if not copy.landed:
                    copy.land()
        rows = pl.ds(first, count)
        total = dot(gall[q, rows], w_cols(n, hi, core, every)[...])
        for k in range(1, 4):
            at = (q + k) % 4
            total += dot(gall[at, rows], wbuf[n, at])
        pbuf[n, rows] = total

    turns = []
    for way in range(2):
        near, far = (way, 2 + way), (1 - way, 3 - way)
        turn = [((r + way) % 2, r) for r in range(4)] + [(1, r) for r in near]
        for step in (2, 3):
            turn += [(step, r) for r in far + near]
        turns.append(turn)
    sums = {}
    ahead = {6: (2, 6), 10: (1, 7)}
    for n in range(len(turns[0])):
        if n == 0:
            hand_on(0)
        if n < 4:
            beside[n].land()
            passed[n].land()
        for far in ahead.get(n, ()):
            partial(far, 0, POS)
        for way, near in ((0, 1), (1, RING - 1)):
            step, r = turns[way][n]
            far = 4 - step if way == 0 else 4 + step
            if n < 6:
                partial(far, r * PIECE, PIECE)
            if way == 1 and n < 3:
                hand_on(n + 1)
            rows = pl.ds(r * PIECE, PIECE)
            total = pbuf[ORDER.index(far), rows]
            if (way, step - 1, r) in sums:
                sums[way, step - 1, r].land()
                total = total + rrecv[way, step - 1, rows].astype(F32)
            rsend[way, step, rows] = total.astype(BF16)
            sums[way, step, r] = remote(
                rsend.at[way, step, rows],
                rrecv.at[way, step, rows],
                r_ss.at[way, step, r],
                r_rs.at[way, step, r],
                (i, ((z + near) % RING) * 4 + q),
            )
    partial(0, 0, POS)
    for r in (1, 3, 0, 2):
        rows = pl.ds(r * PIECE, PIECE)
        total = pbuf[ORDER.index(0), rows]
        for way in range(2):
            sums[way, 3, r].land()
            total = total + rrecv[way, 3, rows].astype(F32)
        out[rows, :] = total.astype(BF16)

    for copy in log:
        copy.leave()


def body(gate, key, value, filt, skip, w, fwd, bwd):
    vmem = pl.BlockSpec(memory_space=pltpu.VMEM)
    hbm = pl.BlockSpec(memory_space=pltpu.HBM)
    dma = pltpu.SemaphoreType.DMA
    return pl.pallas_call(
        kernel,
        out_shape=pltpu.VMEM((POS, CHAN), BF16),
        in_specs=[hbm] * 4 + [vmem] + [hbm] * 3,
        out_specs=vmem,
        scratch_shapes=[
            pltpu.VMEM((POS, CHAN), BF16),
            pltpu.VMEM((POS, CHAN), BF16),
            pltpu.VMEM((POS, CHAN), BF16),
            pltpu.VMEM((POS, CHAN), F32),
            pltpu.VMEM((2 * BLOCK, 2 * BLOCK), BF16),
            pltpu.VMEM((2 * BLOCK, BLOCK), BF16),
            pltpu.VMEM((CHAN, RING * 4 * CHAN), BF16),
            pltpu.VMEM((2, CHAN, POS), BF16),
            pltpu.VMEM((2, CTX, SUB, POS), BF16),
            pltpu.VMEM((2, CHAN, 2 * BLOCK), F32),
            pltpu.VMEM((2, CHAN, 2 * BLOCK), F32),
            pltpu.VMEM((2, CHAN, 2 * BLOCK), F32),
            pltpu.VMEM((2, CHAN, BLOCK), BF16),
            pltpu.VMEM((2, CHAN, BLOCK), BF16),
            pltpu.VMEM((4, POS, CHAN), BF16),
            pltpu.VMEM((RING, 4, CHAN, CHAN), BF16),
            pltpu.VMEM((RING, POS, CHAN), F32),
            pltpu.VMEM((2, 4, POS, CHAN), BF16),
            pltpu.VMEM((2, 4, POS, CHAN), BF16),
            dma((2, CTX - 1)),
            dma((2, CTX - 1)),
            dma((2, CTX - 1)),
            dma((2, CTX - 1)),
            dma((4, 3)),
            dma((4, 3)),
            dma((RING,)),
            dma((RING,)),
            dma((RING, 2, 2)),
            dma((RING, 2, 2)),
            dma((5, 3)),
            dma((5, 3)),
            dma((2, 4, POS // PIECE)),
            dma((2, 4, POS // PIECE)),
            dma((4,)),
            dma((7,)),
        ],
        compiler_params=pltpu.CompilerParams(
            collective_id=0, has_side_effects=True, vmem_limit_bytes=64 * 1024 * 1024 - 1024 * 1024
        ),
        name="hyena",
    )(gate, key, value, filt, skip.reshape(1, CHAN), w, fwd, bwd)


def solution(mesh):
    mapped = jax.shard_map(
        body,
        mesh=mesh,
        in_specs=(P("ctx", "ch"),) * 4 + (P("ch"), P("ch", None), P(), P()),
        out_specs=P("ctx", "ch"),
        check_vma=False,
    )

    def run(out_gate, key_proj, value_proj, filters, skip_gain, out_weight):
        return mapped(out_gate, key_proj, value_proj, filters, skip_gain, out_weight, *tables())

    return run
```
